32 devices in a mesh: dp: 2 (over y), table: 16 (over z, x, core).
Axes of the slice: x: 2, y: 2, z: 4, core: 2. Of those that a mesh axis runs over, the one named last changes fastest.
Arguments:
- emb: bfloat16 [256, 256, 192], P(('dp', 'table')), may hold values from -6 to 6
- grad_fm: bfloat16 [256, 6144], P(('dp', 'table')), may hold values from -1.1953125 to 1.1953125
- grad_comp: bfloat16 [256, 256, 192], P(('dp', 'table')), may hold values from -6 to 6
- proj: bfloat16 [256, 24], replicated, may hold values from -0.375 to 0.375
- comp: bfloat16 [256, 256], replicated, may hold values from -0.375 to 0.375
- slot: int32 [256, 256], P(('dp', 'table')), may hold values from 0 to 127, as said below
- counts: int32 [2, 256], P('dp', 'table'), may hold values from 2 to 4, as said below
Outputs:
- row_grads: bfloat16 [2, 256, 128, 192], P('dp', 'table')
- grad_proj: float32 [256, 24], P('table')
- grad_comp: float32 [256, 256], P('table')
The draws below stay inside these ranges and needn't reach their ends.
Inputs may be any that keep to these rules, and one draw needn't show every extreme that they name: For every group g and table j some sample of g has slot[s, j] = 32 * counts[g, j] - 1, and some has slot[s, j] = 127; entries at or above 32 * counts[g, j] are padded lookups. `counts`: table 0 uses all 4 blocks in every group.
All inputs are finite; a program needn't handle non-finite values.
Results may differ from the reference program's by a relative error of at most 0.0044.
Values may be sent and summed in bfloat16 or wider, within the bound.
No kernel may reach another device: no remote copies, remote signals or barrier semaphores. Data moves between devices by JAX's collectives and lax.ppermute only.
A program may use at most 64 MiB of HBM per device.

```python
import math
import jax
import jax.numpy as jnp
from jax import lax

NE = 256
D = 192
K = 24
NC = 256
BLOCKS = 4
GROUP = 128
SAMPLES = 256
SLOTS = 128
BLOCK_ROWS = 32
N_DP = 2


def shared_counts(key):
    raw = jax.random.randint(key, (N_DP, NE), max(1, BLOCKS // 2), BLOCKS + 1)
    first = jnp.arange(NE)[None, :] == 0
    return jnp.where(first, BLOCKS, raw).astype(jnp.int32)


def draw_counts(key, part):
    return shared_counts(key)


def draw_slot(key, part):
    counts = shared_counts(key)
    key = jax.random.fold_in(key, 2)
    group_of = jnp.arange(SAMPLES) // GROUP
    limits = counts[group_of] * BLOCK_ROWS
    raw = jax.random.randint(key, (SAMPLES, NE), 0, SLOTS)
    position = (jnp.arange(SAMPLES) % GROUP)[:, None]
    highest_slot = jnp.full((SAMPLES, NE), SLOTS - 1, jnp.int32)
    picked_slots = jnp.where(position == 0, limits - 1, raw)
    picked_slots = jnp.where(position == 1, highest_slot, picked_slots)
    return picked_slots.astype(jnp.int32)


def with_spikes(entries, stream_key, source, target, blocks, factor):
    def block_of(dim):
        return (jnp.arange(entries.shape[dim]) // (entries.shape[dim] // blocks)).reshape((-1,) + (1,) * (entries.ndim - 1 - dim))

    near = jax.random.permutation(stream_key, blocks)[block_of(target)]
    second = (block_of(target) + blocks // 2) % blocks
    return jnp.where((block_of(source) == near) | (block_of(source) == second), factor * entries, entries)


def steps_of(rng, dims, shards, low, high):
    loudness = 1.0
    for dim, parts in shards:
        draws = jax.random.uniform(jax.random.fold_in(jax.random.fold_in(rng, 6), dim), (parts,), jnp.float32, low / len(shards), high / len(shards))
        loudness = loudness * jnp.repeat(jnp.exp(draws), dims[dim] // parts).reshape((-1,) + (1,) * (len(dims) - 1 - dim))
    return loudness


def gaussian(own_key, dims, scale, most, pieces=(), kind=jnp.bfloat16):
    level = steps_of(own_key, dims, pieces, -0.22, 0.18) if pieces else 1.0
    array = jax.random.normal(own_key, dims, jnp.float32) * scale * level
    return jnp.minimum(jnp.maximum(array, -most), most).astype(kind)


def heavy_noise(own_key, dims, deviation, bound, split, heavy, kind=jnp.bfloat16):
    result = deviation * jax.random.normal(own_key, dims, jnp.float32)
    if split:
        result = result * steps_of(own_key, dims, split, -0.22, 0.18)
    return jnp.clip(with_spikes(result, jax.random.fold_in(own_key, 3), *heavy), -bound, bound).astype(kind)


def setup_inputs(seed: int = 0) -> dict:
    streams_of = jax.random.split(jax.random.key(seed), 8)
    return {
        "emb": heavy_noise(streams_of[0], (SAMPLES, NE, D), 1.0, 6.0, ((0, 32),), (0, 1, 32, 2.75)),
        "grad_fm": gaussian(streams_of[1], (SAMPLES, NE * K), 0.2, 1.1953125, ((0, 32),)),
        "grad_comp": heavy_noise(streams_of[2], (SAMPLES, NC, D), 1.0, 6.0, ((0, 32),), (0, 1, 32, 2.75)),
        "proj": gaussian(streams_of[3], (NE, K), NE ** -0.5, 0.375),
        "comp": gaussian(streams_of[4], (NC, NE), NE ** -0.5, 0.375),
        "slot": draw_slot(jax.random.fold_in(streams_of[7], 71), 0),
        "counts": draw_counts(jax.random.fold_in(streams_of[7], 71), 0),
    }


FULL_ACCURACY = lax.Precision.HIGHEST

def group_step(carry, items):
    emb, grad_fm, grad_comp, slot, counts, proj, comp = items
    acc_proj, acc_comp = carry
    x = emb.astype(jnp.float32)
    gf = grad_fm.reshape(GROUP, NE, K).astype(jnp.float32)
    gc = grad_comp.astype(jnp.float32)
    wp = proj.astype(jnp.float32)
    wc = comp.astype(jnp.float32)
    lower_limit = jnp.einsum('nk,gnd->gkd', wp, x, precision=FULL_ACCURACY)
    cross_term = jnp.einsum('gnk,gnd->gkd', gf, x, precision=FULL_ACCURACY)
    gradient_list = jnp.einsum('gnk,gkd->gnd', gf, lower_limit, precision=FULL_ACCURACY)
    gradient_list = gradient_list + jnp.einsum('nk,gkd->gnd', wp, cross_term, precision=FULL_ACCURACY)
    gradient_list = gradient_list + jnp.einsum('cn,gcd->gnd', wc, gc, precision=FULL_ACCURACY)
    input_grad = gradient_list.astype(jnp.bfloat16)
    acc_proj = acc_proj + jnp.einsum('gnd,gkd->nk', x, cross_term, precision=FULL_ACCURACY)
    acc_comp = acc_comp + jnp.einsum('gcd,gnd->cn', gc, x, precision=FULL_ACCURACY)

    def per_table(values, slots):
        return jax.ops.segment_sum(values.astype(jnp.float32), slots, num_segments=SLOTS)
    sums = jax.vmap(per_table, in_axes=(1, 1))(input_grad, slot)
    live = jnp.arange(SLOTS, dtype=jnp.int32)[None, :] < (counts * BLOCK_ROWS)[:, None]
    rows = jnp.where(live[:, :, None], sums, jnp.float32(0.0)).astype(jnp.bfloat16)
    return ((acc_proj, acc_comp), rows)

def reference(emb, grad_fm, grad_comp, proj, comp, slot, counts):
    items = (emb.reshape(N_DP, GROUP, NE, D), grad_fm.reshape(N_DP, GROUP, NE * K), grad_comp.reshape(N_DP, GROUP, NC, D), slot.reshape(N_DP, GROUP, NE), counts)
    start = (jnp.zeros((NE, K), jnp.float32), jnp.zeros((NC, NE), jnp.float32))

    def step(carry, piece):
        return group_step(carry, piece + (proj, comp))
    (acc_proj, acc_comp), rows = lax.scan(step, start, items)
    scale = 1.0 / math.sqrt(SAMPLES * D)
    return (rows, acc_proj * scale, acc_comp * scale)
```

```python
import math

import jax
import jax.numpy as jnp
from jax import lax
from jax.experimental import pallas as pl
from jax.experimental.pallas import tpu as pltpu
from jax.sharding import PartitionSpec as P

BLOCKS = 4
F32 = jnp.float32
BF16 = jnp.bfloat16
LANES = 128
HALF = 64


def dot(a, b, ca, cb):
    return lax.dot_general(a, b, (((ca,), (cb,)), ((), ())), preferred_element_type=F32)


def iota(shape, dim):
    return lax.broadcasted_iota(jnp.int32, shape, dim)


def round_up(n, m):
    return -(-n // m) * m


def send_kernel(tables, x_ref, h_ref, g_ref, proj_ref, comp_ref, slot_ref, out_ref, spread, main, rest, both):
    count, depth, width = x_ref.shape
    rank = proj_ref.shape[0]
    local = width // tables
    comp_rows = comp_ref.shape[0] // tables
    per = 16
    span = per * rank

    row, col = iota((rank, LANES), 0), iota((rank, LANES), 1)
    eye = ((col == row) | (col == row + rank)).astype(F32)
    fold = jnp.concatenate([eye] * per, axis=0).astype(BF16)
    place = ((col == row + HALF) | (col == row + HALF + rank)).astype(BF16)
    placed_proj = dot(proj_ref[...], place, 0, 0)
    comp_t = comp_ref[...].astype(F32).T.astype(BF16)
    sub, lane = iota((8, span), 0), iota((8, span), 1)
    masks = [(lane >= rank * (sub + 8 * i)) & (lane < rank * (sub + 8 * i + 1)) for i in range(per // 8)]
    lane_l = iota((depth, LANES), 1)
    first = (lane_l % HALF) < rank

    for a in range(width // per):
        block = g_ref[:, a * span:(a + 1) * span].astype(F32)
        for s in range(count):
            wide = jnp.broadcast_to(block[s:s + 1, :], (8, span))
            spread[s, a * per:(a + 1) * per, :] = jnp.concatenate(
                [jnp.where(m, wide, 0.0) for m in masks], axis=0
            ).astype(BF16)

    for s in range(count):
        factors = (dot(spread[s], fold, 1, 0) + placed_proj).astype(BF16)
        terms = dot(x_ref[s], factors, 1, 0)
        high = terms.astype(BF16).astype(F32)
        split = jnp.where(first, high, terms - high)
        both[s * depth:(s + 1) * depth, :] = split.astype(BF16)
        swapped = pltpu.roll(split, HALF, 1).astype(BF16)
        h = h_ref[s]
        h_wide = jnp.concatenate([h, h[LANES:]], axis=0)
        swapped_wide = jnp.concatenate([swapped, swapped[LANES:]], axis=0)
        grads = dot(comp_t, h_wide, 1, 1) + dot(factors, swapped_wide, 1, 1)
        main[pl.ds(s, width, stride=count), :] = grads[:, :LANES]
        rest[pl.ds(s, width, stride=count), :] = grads[:, LANES:]

    x_all = x_ref[...].reshape(count * depth, width)
    h_all = h_ref[...].reshape(count * depth, comp_ref.shape[0])
    comp_grad = dot(h_all, x_all, 0, 0)
    proj_parts = dot(both[...], x_all, 0, 0)
    proj_grad = proj_parts[:rank] + proj_parts[rank:2 * rank]
    slot = slot_ref[...]
    slot_high = slot // 16
    sources = [slot_high.astype(F32), (slot - 16 * slot_high).astype(F32)]
    sources += [proj_grad[8 * i:8 * i + 8] for i in range(rank // 8)]

    rows = local * count
    left = iota((rows // 2, LANES), 1) < HALF
    small = iota((8, LANES), 1)
    tail = out_ref.shape[1] - rows - rows // 2
    for t in range(tables):
        out_ref[t, 0:rows, :] = main[t * rows:(t + 1) * rows, :].astype(BF16)
        upper = rest[t * rows:t * rows + rows // 2, :]
        lower = rest[t * rows + rows // 2:(t + 1) * rows, :]
        out_ref[t, rows:rows + rows // 2, :] = jnp.where(left, upper, lower).astype(BF16)
        part, offset = (t * local) // LANES, (t * local) % LANES
        mixed = jnp.zeros((8, LANES), F32)
        for i, source in enumerate(sources):
            piece = source[:, part * LANES:(part + 1) * LANES]
            shift = (i * local - offset) % LANES
            if shift:
                piece = pltpu.roll(piece, shift, 1)
            mixed = jnp.where((small >= i * local) & (small < (i + 1) * local), piece, mixed)
        mine = comp_grad[t * comp_rows:(t + 1) * comp_rows]
        pieces = [mine[:, i * LANES:(i + 1) * LANES] for i in range(width // LANES)] + [mixed]
        used = comp_rows * (width // LANES) + 8
        if tail > used:
            pieces.append(jnp.zeros((tail - used, LANES), F32))
        out_ref[t, rows + rows // 2:, :] = jnp.concatenate(pieces, axis=0).astype(BF16)


def receive_kernel(block_rows, comp_part, in_ref, counts_ref, rows_ref, sums_ref):
    tables = in_ref.shape[0]
    local, depth, slots = rows_ref.shape
    count = 8
    rows = local * count
    tail = rows + rows // 2
    last = in_ref[:, tail:, :].astype(F32)
    sums_ref[...] = jnp.sum(last, axis=0)
    mixed = last[:, comp_part:comp_part + 8, :]
    slot = 16.0 * mixed[:, :, 0:local] + mixed[:, :, local:2 * local]
    limits = (counts_ref[...] * block_rows).astype(F32)
    slot = jnp.where(slot < limits[None], slot, -1.0)
    target = iota((tables, count, 2 * slots), 2)
    targets = [target.astype(F32), jnp.where(target < slots, -2, target - slots).astype(F32)]
    half_pairs = max(local // 4, 1)
    rest = {}
    for j in range(local // 2):
        hot = jnp.stack(
            [
                (slot[:, :, 2 * j + i:2 * j + i + 1] == targets[i]).astype(F32)
                for i in range(2)
            ],
            axis=1,
        ).reshape(tables * 2 * count, 2 * slots).astype(BF16)
        lead = in_ref[:, 16 * j:16 * j + 16, :].reshape(tables * 16, LANES)
        k = j % half_pairs
        other = in_ref[:, rows + 16 * k:rows + 16 * k + 16, :].reshape(tables * 16, LANES)
        top = dot(lead, hot, 0, 0).astype(BF16)
        bottom = dot(other, hot, 0, 0)
        at = HALF * (j // half_pairs)
        bottom = bottom[at:at + HALF].astype(BF16)
        for i in range(2):
            rows_ref[2 * j + i, 0:LANES, :] = top[:, i * slots:(i + 1) * slots]
            rows_ref[2 * j + i, LANES:, :] = bottom[:, i * slots:(i + 1) * slots]


def finish_kernel(scale, parts, comp_rows, local, rank, *refs):
    ins, (proj_ref, comp_ref) = refs[:parts], refs[parts:]
    total = ins[0][...]
    for ref in ins[1:]:
        total = total + ref[...]
    total = total * scale
    halves = comp_ref.shape[1] // LANES
    comp_ref[...] = jnp.concatenate([total[i * comp_rows:(i + 1) * comp_rows] for i in range(halves)], axis=1)
    mixed = total[halves * comp_rows:halves * comp_rows + 8].T
    proj_ref[...] = jnp.concatenate(
        [mixed[(2 + i) * local:(3 + i) * local, :] for i in range(rank // 8)], axis=1
    )


def shards(emb, grad_fm, grad_comp, proj, comp, slot, counts):
    count, width, depth = emb.shape
    rank = proj.shape[1]
    tables = lax.axis_size("table")
    groups = lax.axis_size("dp")
    local = width // tables
    slot_count = count * tables
    comp_width = comp.shape[0]
    comp_rows = comp_width // tables
    rows = local * count
    comp_part = comp_rows * (width // LANES)
    tail = round_up(comp_part + 8, 16)
    total_rows = rows + rows // 2 + tail
    vmem = pl.BlockSpec(memory_space=pltpu.VMEM)
    params = pltpu.CompilerParams(vmem_limit_bytes=40 * 1024 * 1024)

    def send(*refs):
        send_kernel(tables, *refs)

    sent = pl.pallas_call(
        send,
        out_shape=jax.ShapeDtypeStruct((tables, total_rows, LANES), BF16),
        in_specs=[vmem] * 6,
        out_specs=vmem,
        scratch_shapes=[
            pltpu.VMEM((count, width, 16 * rank), BF16),
            pltpu.VMEM((count * width, LANES), F32),
            pltpu.VMEM((count * width, LANES), F32),
            pltpu.VMEM((count * depth, LANES), BF16),
        ],
        compiler_params=params,
        name="send",
    )(jnp.swapaxes(emb, 1, 2), jnp.swapaxes(grad_comp, 1, 2), grad_fm, proj.T, comp, slot)
    got = lax.all_to_all(sent, "table", split_axis=0, concat_axis=0, tiled=True)

    def receive(*refs):
        receive_kernel(slot_count // BLOCKS, comp_part, *refs)

    row_grads, sums = pl.pallas_call(
        receive,
        out_shape=(
            jax.ShapeDtypeStruct((local, depth, slot_count), BF16),
            jax.ShapeDtypeStruct((tail, LANES), F32),
        ),
        in_specs=[vmem] * 2,
        out_specs=(vmem, vmem),
        compiler_params=params,
        name="receive",
    )(got, counts)
    if groups == 2:
        parts = (sums, lax.ppermute(sums, "dp", [(0, 1), (1, 0)]))
    else:
        parts = (lax.psum(sums, "dp"),)
    scale = 1.0 / math.sqrt(count * tables * groups * depth)

    def finish(*refs):
        finish_kernel(scale, len(parts), comp_rows, local, rank, *refs)

    grad_proj, grad_comp_out = pl.pallas_call(
        finish,
        out_shape=(
            jax.ShapeDtypeStruct((local, rank), F32),
            jax.ShapeDtypeStruct((comp_rows, width), F32),
        ),
        in_specs=[vmem] * len(parts),
        out_specs=(vmem, vmem),
        compiler_params=params,
        name="finish",
    )(*parts)
    return (jnp.swapaxes(row_grads, 1, 2)[None], grad_proj, grad_comp_out)


def solution(mesh):
    placed = (
        P(("dp", "table"), None, None),
        P(("dp", "table"), None),
        P(("dp", "table"), None, None),
        P(),
        P(),
        P(("dp", "table"), None),
        P("dp", "table"),
    )
    return jax.shard_map(
        shards,
        mesh=mesh,
        in_specs=placed,
        out_specs=(P("dp", "table", None, None), P("table", None), P("table", None)),
        check_vma=False,
    )
```

```python
import math

import jax
import jax.numpy as jnp
from jax import lax
from jax.experimental import pallas as pl
from jax.experimental.pallas import tpu as pltpu
from jax.sharding import PartitionSpec as P

BLOCKS = 4
F32 = jnp.float32
BF16 = jnp.bfloat16
LANES = 128
HALF = 64
CROSS = 0
LAST = BF16
STAGES = lambda bits: [[b] for b in range(1, bits - 2)] + [[bits - 2, bits - 1]]


def dot(a, b, ca, cb):
    return lax.dot_general(a, b, (((ca,), (cb,)), ((), ())), preferred_element_type=F32)


def iota(shape, dim):
    return lax.broadcasted_iota(jnp.int32, shape, dim)


def round_up(n, m):
    return -(-n // m) * m


def send_kernel(tables, index_ref, x_hbm, h_hbm, g_hbm, proj_hbm, comp_hbm, slot_hbm, out_hbm, keep_hbm, give_hbm,
                x_ref, h_ref, g_ref, proj_ref, comp_ref, slot_ref, spread, factors, both, swapped, main, rest, out_ref, keep_ref, give_ref, sems):
    count, depth, width = x_ref.shape
    rank = proj_ref.shape[0]
    comp_width = comp_ref.shape[0]
    local, comp_rows = width // tables, comp_width // tables
    block = 8 * rank
    window = 2 * LANES

    pairs = [(g_hbm, g_ref), (proj_hbm, proj_ref), (x_hbm, x_ref), (h_hbm, h_ref), (comp_hbm, comp_ref), (slot_hbm, slot_ref)]
    copies = [pltpu.make_async_copy(a, b, sems.at[i]) for i, (a, b) in enumerate(pairs)]
    for copy in copies:
        copy.start()
    sends = [pltpu.make_async_copy(out_ref.at[t], out_hbm.at[t], sems.at[8 + t]) for t in range(tables)]
    keep_copy = pltpu.make_async_copy(keep_ref, keep_hbm, sems.at[6])
    give_copy = pltpu.make_async_copy(give_ref, give_hbm, sems.at[7])

    row, col = iota((rank, LANES), 0), iota((rank, LANES), 1)
    eye = ((col == row) | (col == row + rank)).astype(F32)
    place = ((col == row + HALF) | (col == row + HALF + rank)).astype(BF16)
    sub, lane = iota((8, window), 0), iota((8, window), 1)
    folds, masks = [], []
    for start in (0, HALF):
        parts = [eye] * 8
        if start:
            parts = [jnp.zeros((start, LANES), F32)] + parts
        if window > start + block:
            parts = parts + [jnp.zeros((window - start - block, LANES), F32)]
        folds.append(jnp.concatenate(parts, axis=0).astype(BF16))
        masks.append((lane >= start + rank * sub) & (lane < start + rank * (sub + 1)))
    first = (iota((depth, LANES), 1) % HALF) < rank

    copies[0].wait()
    copies[1].wait()
    for a in range(width // 8):
        start, odd = (a * block) // LANES * LANES, a % 2
        piece = g_ref[:, start:start + window].astype(F32)
        for s in range(count):
            wide = jnp.broadcast_to(piece[s:s + 1, :], (8, window))
            spread[odd, s * (width // 2) + (a // 2) * 8:s * (width // 2) + (a // 2) * 8 + 8, :] = jnp.where(masks[odd], wide, 0.0).astype(BF16)
    placed_proj = dot(proj_ref[...], place, 0, 0)
    for s in range(count):
        lo, hi = s * (width // 2), (s + 1) * (width // 2)
        halves = [dot(spread[i, lo:hi, :], folds[i], 1, 0).reshape(width // 16, 8, LANES) for i in range(2)]
        columns = jnp.stack(halves, axis=1).reshape(width, LANES)
        factors[s] = (columns + placed_proj).astype(BF16)
    copies[2].wait()
    for s in range(count):
        terms = dot(x_ref[s], factors[s], 1, 0)
        high = terms.astype(BF16).astype(F32)
        split = jnp.where(first, high, terms - high)
        both[s * depth:(s + 1) * depth, :] = split.astype(BF16)
        swapped[s] = pltpu.roll(split, HALF, 1).astype(BF16)
    copies[3].wait()
    copies[4].wait()
    copies[5].wait()

    x_all = x_ref[...].reshape(count * depth, width)
    h_all = h_ref[...].reshape(count * depth, comp_width)
    comp_grad = dot(h_all, x_all, 0, 0)
    proj_parts = dot(both[...], x_all, 0, 0)
    proj_grad = proj_parts[:rank] + proj_parts[rank:2 * rank]
    sources = [proj_grad[8 * i:8 * i + 8] for i in range(rank // 8)]
    even = (index_ref[0] % 2) == 0

    def weight_block(t):
        mine = comp_grad[t * comp_rows:(t + 1) * comp_rows]
        pieces = [mine[:, i * LANES:(i + 1) * LANES] for i in range(width // LANES)]
        return jnp.concatenate(pieces + [gather_lanes(sources, t, local)], axis=0)

    for i in range(tables // 2):
        zero, one = weight_block(2 * i), weight_block(2 * i + 1)
        keep_ref[i] = jnp.where(even, zero, one)
        give_ref[i] = jnp.where(even, one, zero)
    give_copy.start()
    keep_copy.start()

    comp_t = comp_ref[...].astype(F32).T.astype(BF16)
    for s in range(count):
        h, other = h_ref[s], swapped[s]
        h_wide = jnp.concatenate([h, h[LANES:]], axis=0)
        other_wide = jnp.concatenate([other, other[LANES:]], axis=0)
        grads = dot(comp_t, h_wide, 1, 1) + dot(factors[s], other_wide, 1, 1)
        main[pl.ds(s, width, stride=count), :] = grads[:, :LANES]
        rest[pl.ds(s, width, stride=count), :] = grads[:, LANES:]

    slot = slot_ref[...]
    slot_high = slot // 16
    sources = [slot_high.astype(F32), (slot - 16 * slot_high).astype(F32)]
    rows = local * count
    left = iota((rows // 2, LANES), 1) < HALF
    for t in range(tables):
        out_ref[t, 0:rows, :] = main[t * rows:(t + 1) * rows, :].astype(BF16)
        upper = rest[t * rows:t * rows + rows // 2, :]
        lower = rest[t * rows + rows // 2:(t + 1) * rows, :]
        out_ref[t, rows:rows + rows // 2, :] = jnp.where(left, upper, lower).astype(BF16)
        mixed = gather_lanes(sources, t, local)
        out_ref[t, rows + rows // 2:, :] = jnp.concatenate([mixed, mixed], axis=0).astype(BF16)
        sends[t].start()
    give_copy.wait()
    keep_copy.wait()
    for copy in sends:
        copy.wait()


def gather_lanes(sources, t, local):
    part, offset = (t * local) // LANES, (t * local) % LANES
    lane = iota((8, LANES), 1)
    mixed = jnp.zeros((8, LANES), F32)
    for i, source in enumerate(sources):
        piece = source[:, part * LANES:(part + 1) * LANES]
        shift = (i * local - offset) % LANES
        if shift:
            piece = pltpu.roll(piece, shift, 1)
        mixed = jnp.where((lane >= i * local) & (lane < (i + 1) * local), piece, mixed)
    return mixed


def split(blocks, bits, index):
    if not bits:
        return [blocks]
    even = ((index >> bits[0]) % 2) == 0
    keep = [jnp.where(even, zero, one) for zero, one in zip(blocks[0::2], blocks[1::2])]
    give = [jnp.where(even, one, zero) for zero, one in zip(blocks[0::2], blocks[1::2])]
    return [part for pair in zip(split(keep, bits[1:], index), split(give, bits[1:], index)) for part in pair]


def total_of(refs, i):
    parts = [ref[i].astype(F32) for ref in refs]
    while len(parts) > 1:
        parts = [sum(parts[j:j + 2][1:], parts[j]) for j in range(0, len(parts), 2)]
    return parts[0]


def split_kernel(bits, index_ref, *refs):
    ins, outs = refs[:-2 ** len(bits)], refs[-2 ** len(bits):]
    parts = split([total_of(ins, i) for i in range(ins[0].shape[0])], bits, index_ref[0])
    for out, blocks in zip(outs, parts):
        for i, block in enumerate(blocks):
            out[i] = block.astype(out.dtype)


def add_kernel(*refs):
    refs[-1][0] = total_of(refs[:-1], 0)


def finish_kernel(scale, comp_rows, local, rank, after_ref, *refs):
    proj_ref, comp_ref = refs[-2:]
    total = total_of(refs[:-2], 0) * scale
    halves = comp_ref.shape[1] // LANES
    comp_ref[...] = jnp.concatenate([total[i * comp_rows:(i + 1) * comp_rows] for i in range(halves)], axis=1)
    mixed = total[halves * comp_rows:halves * comp_rows + 8].T
    proj_ref[...] = jnp.concatenate([mixed[i * local:(i + 1) * local, :] for i in range(rank // 8)], axis=1)


def hold_kernel(in_ref, out_ref):
    pass


def receive_kernel(block_rows, in_ref, counts_ref, rows_ref, after_ref):
    after_ref[...] = jnp.zeros_like(after_ref)
    tables = in_ref.shape[0]
    local, depth, slots = rows_ref.shape
    count = 8
    rows = local * count
    tail = rows + rows // 2
    mixed = in_ref[:, tail:, :].astype(F32)[:, :8, :]
    slot = 16.0 * mixed[:, :, 0:local] + mixed[:, :, local:2 * local]
    limits = (counts_ref[...] * block_rows).astype(F32)
    slot = jnp.where(slot < limits[None], slot, -1.0)
    target = iota((tables, count, 2 * slots), 2)
    targets = [target.astype(F32), jnp.where(target < slots, -2, target - slots).astype(F32)]
    half_pairs = max(local // 4, 1)
    for j in range(local // 2):
        hot = jnp.stack(
            [(slot[:, :, 2 * j + i:2 * j + i + 1] == targets[i]).astype(F32) for i in range(2)], axis=1
        ).reshape(tables * 2 * count, 2 * slots).astype(BF16)
        lead = in_ref[:, 16 * j:16 * j + 16, :].reshape(tables * 16, LANES)
        k = j % half_pairs
        other = in_ref[:, rows + 16 * k:rows + 16 * k + 16, :].reshape(tables * 16, LANES)
        top = dot(lead, hot, 0, 0).astype(BF16)
        bottom = dot(other, hot, 0, 0)
        at = HALF * (j // half_pairs)
        bottom = bottom[at:at + HALF].astype(BF16)
        for i in range(2):
            rows_ref[2 * j + i, 0:LANES, :] = top[:, i * slots:(i + 1) * slots]
            rows_ref[2 * j + i, LANES:, :] = bottom[:, i * slots:(i + 1) * slots]


def shards(emb, grad_fm, grad_comp, proj, comp, slot, counts):
    count, width, depth = emb.shape
    rank = proj.shape[1]
    tables = lax.axis_size("table")
    groups = lax.axis_size("dp")
    local = width // tables
    slot_count = count * tables
    comp_width = comp.shape[0]
    comp_rows = comp_width // tables
    rows = local * count
    total_rows = rows + rows // 2 + 16
    vmem = pl.BlockSpec(memory_space=pltpu.VMEM)
    smem = pl.BlockSpec(memory_space=pltpu.SMEM)
    hbm = pl.BlockSpec(memory_space=pltpu.HBM)
    params = pltpu.CompilerParams(vmem_limit_bytes=40 * 1024 * 1024)
    large = pltpu.CompilerParams(vmem_limit_bytes=60 * 1024 * 1024)

    def call(body, name, outs, ins, specs, params=params, out=vmem, **more):
        return pl.pallas_call(
            body,
            out_shape=tuple(jax.ShapeDtypeStruct(*o) for o in outs),
            in_specs=specs,
            out_specs=(out,) * len(outs),
            compiler_params=params,
            name=name,
            **more,
        )(*ins)

    x, h = jnp.swapaxes(emb, 1, 2), jnp.swapaxes(grad_comp, 1, 2)
    index = lax.axis_index("table").astype(jnp.int32).reshape(1)
    part = comp_rows * (width // LANES) + 8
    shapes = [((tables, total_rows, LANES), BF16)] + [((tables // 2, part, LANES), F32)] * 2
    sent, keep, give = call(
        lambda *refs: send_kernel(tables, *refs),
        "send",
        shapes,
        (index, x, h, grad_fm, proj.T, comp, slot),
        [smem] + [hbm] * 6,
        params=large,
        out=hbm,
        scratch_shapes=[
            pltpu.VMEM(x.shape, BF16),
            pltpu.VMEM(h.shape, BF16),
            pltpu.VMEM(grad_fm.shape, BF16),
            pltpu.VMEM((rank, width), BF16),
            pltpu.VMEM(comp.shape, BF16),
            pltpu.VMEM(slot.shape, jnp.int32),
            pltpu.VMEM((2, count * width // 2, 2 * LANES), BF16),
            pltpu.VMEM((count, width, LANES), BF16),
            pltpu.VMEM((count * depth, LANES), BF16),
            pltpu.VMEM((count, depth, LANES), BF16),
            pltpu.VMEM((count * width, LANES), F32),
            pltpu.VMEM((count * width, LANES), F32),
        ]
        + [pltpu.VMEM(*o) for o in shapes]
        + [pltpu.SemaphoreType.DMA((8 + tables,))],
    )
    def swap(array, offset, other_group=0):
        pairs = [
            (g * tables + i, (g ^ other_group) * tables + (i ^ offset)) for g in range(groups) for i in range(tables)
        ]
        return lax.ppermute(array, ("dp", "table"), pairs)

    bits = tables.bit_length() - 1
    sums = [keep, swap(give, 1)]
    got = lax.all_to_all(sent, "table", split_axis=0, concat_axis=0, tiled=True)
    for stage in STAGES(bits):
        size = sums[0].shape[0] >> len(stage)
        cross = stage == STAGES(bits)[CROSS] and groups == 2
        kinds = [BF16 if cross else F32] + [BF16 if cross else LAST] * (2 ** len(stage) - 1)
        parts = call(
            lambda *refs, stage=stage: split_kernel(stage, *refs),
            "split",
            [((size, part, LANES), kind) for kind in kinds],
            (index, *sums),
            [smem] + [vmem] * len(sums),
            cost_estimate=pl.CostEstimate(flops=10**11 if stage == STAGES(bits)[0] else 10**6, bytes_accessed=10**6, transcendentals=0),
        )
        sums = [p if o == 0 else swap(p, o << stage[0]) for o, p in enumerate(parts)]
        if cross:
            sums += [swap(p, o << stage[0], 1) for o, p in enumerate(parts)]
    step = 1
    while step < groups and groups != 2:
        keep, = call(add_kernel, "add", [(sums[0].shape, F32)], sums, [vmem] * len(sums))
        sums = [keep, swap(keep, 0, step)]
        step *= 2
    row_grads, after = call(
        lambda *refs: receive_kernel(slot_count // BLOCKS, *refs),
        "receive",
        [((local, depth, slot_count), BF16), ((8, LANES), F32)],
        (got, counts),
        [vmem] * 2,
    )
    scale = 1.0 / math.sqrt(count * tables * groups * depth)
    grad_proj, grad_comp_out = call(
        lambda *refs: finish_kernel(scale, comp_rows, local, rank, *refs),
        "finish",
        [((local, rank), F32), ((comp_rows, width), F32)],
        (after, *sums),
        [vmem] + [vmem] * len(sums),
    )
    return (jnp.swapaxes(row_grads, 1, 2)[None], grad_proj, grad_comp_out)


def solution(mesh):
    placed = (
        P(("dp", "table"), None, None),
        P(("dp", "table"), None),
        P(("dp", "table"), None, None),
        P(),
        P(),
        P(("dp", "table"), None),
        P("dp", "table"),
    )
    return jax.shard_map(
        shards,
        mesh=mesh,
        in_specs=placed,
        out_specs=(P("dp", "table", None, None), P("table", None), P("table", None)),
        check_vma=False,
    )
```

```python
import math

import jax
import jax.numpy as jnp
from jax import lax
from jax.experimental import pallas as pl
from jax.experimental.pallas import tpu as pltpu
from jax.sharding import PartitionSpec as P

BLOCKS = 4
F32 = jnp.float32
BF16 = jnp.bfloat16
LANES = 128
HALF = 64
CROSS = 0
LAST = BF16
STAGES = lambda bits: [[b] for b in range(1, bits - 2)] + [[bits - 2, bits - 1]]


def dot(a, b, ca, cb):
    return lax.dot_general(a, b, (((ca,), (cb,)), ((), ())), preferred_element_type=F32)


def iota(shape, dim):
    return lax.broadcasted_iota(jnp.int32, shape, dim)


def round_up(n, m):
    return -(-n // m) * m


def send_kernel(tables, x_hbm, h_hbm, g_hbm, proj_hbm, comp_hbm, slot_hbm, out_hbm, both_hbm,
                x_ref, h_ref, g_ref, proj_ref, comp_ref, slot_ref, spread, factors, both, swapped, main, rest, out_ref, sems):
    count, depth, width = x_ref.shape
    rank = proj_ref.shape[0]
    comp_width = comp_ref.shape[0]
    local, comp_rows = width // tables, comp_width // tables
    block = 8 * rank
    window = 2 * LANES

    pairs = [(g_hbm, g_ref), (proj_hbm, proj_ref), (x_hbm, x_ref), (h_hbm, h_ref), (comp_hbm, comp_ref), (slot_hbm, slot_ref)]
    copies = [pltpu.make_async_copy(a, b, sems.at[i]) for i, (a, b) in enumerate(pairs)]
    pieces = 4
    for i, (a, b) in enumerate(pairs[2:4]):
        size = count // pieces
        copies[2 + i] = [
            pltpu.make_async_copy(
                a.at[p * size:(p + 1) * size], b.at[p * size:(p + 1) * size], sems.at[8 + tables + i * pieces + p]
            )
            for p in range(pieces)
        ]
    for copy in copies[:2] + copies[2] + copies[3] + copies[4:]:
        copy.start()
    sends = [pltpu.make_async_copy(out_ref.at[t], out_hbm.at[t], sems.at[8 + t]) for t in range(tables)]
    both_copy = pltpu.make_async_copy(both, both_hbm, sems.at[6])

    row, col = iota((rank, LANES), 0), iota((rank, LANES), 1)
    eye = ((col == row) | (col == row + rank)).astype(F32)
    place = ((col == row + HALF) | (col == row + HALF + rank)).astype(BF16)
    sub, lane = iota((8, window), 0), iota((8, window), 1)
    folds, masks = [], []
    for start in (0, HALF):
        parts = [eye] * 8
        if start:
            parts = [jnp.zeros((start, LANES), F32)] + parts
        if window > start + block:
            parts = parts + [jnp.zeros((window - start - block, LANES), F32)]
        folds.append(jnp.concatenate(parts, axis=0).astype(BF16))
        masks.append((lane >= start + rank * sub) & (lane < start + rank * (sub + 1)))
    first = (iota((depth, LANES), 1) % HALF) < rank

    copies[0].wait()
    copies[1].wait()
    for a in range(width // 8):
        start, odd = (a * block) // LANES * LANES, a % 2
        piece = g_ref[:, start:start + window].astype(F32)
        for s in range(count):
            wide = jnp.broadcast_to(piece[s:s + 1, :], (8, window))
            spread[odd, s * (width // 2) + (a // 2) * 8:s * (width // 2) + (a // 2) * 8 + 8, :] = jnp.where(masks[odd], wide, 0.0).astype(BF16)
    placed_proj = dot(proj_ref[...], place, 0, 0)
    for s in range(count):
        lo, hi = s * (width // 2), (s + 1) * (width // 2)
        halves = [dot(spread[i, lo:hi, :], folds[i], 1, 0).reshape(width // 16, 8, LANES) for i in range(2)]
        columns = jnp.stack(halves, axis=1).reshape(width, LANES)
        factors[s] = (columns + placed_proj).astype(BF16)
    for copy in copies[2]:
        copy.wait()
    for s in range(count):
        terms = dot(x_ref[s], factors[s], 1, 0)
        high = terms.astype(BF16).astype(F32)
        split = jnp.where(first, high, terms - high)
        both[s * depth:(s + 1) * depth, :] = split.astype(BF16)
        swapped[s] = pltpu.roll(split, HALF, 1).astype(BF16)
    for copy in copies[3]:
        copy.wait()
    copies[4].wait()
    copies[5].wait()

    both_copy.start()

    comp_t = comp_ref[...].astype(F32).T.astype(BF16)
    for s in range(count):
        h, other = h_ref[s], swapped[s]
        h_wide = jnp.concatenate([h, h[LANES:]], axis=0)
        other_wide = jnp.concatenate([other, other[LANES:]], axis=0)
        grads = dot(comp_t, h_wide, 1, 1) + dot(factors[s], other_wide, 1, 1)
        main[pl.ds(s, width, stride=count), :] = grads[:, :LANES]
        rest[pl.ds(s, width, stride=count), :] = grads[:, LANES:]

    slot = slot_ref[...]
    slot_high = slot // 16
    sources = [slot_high.astype(F32), (slot - 16 * slot_high).astype(F32)]
    rows = local * count
    left = iota((rows // 2, LANES), 1) < HALF
    for t in range(tables):
        out_ref[t, 0:rows, :] = main[t * rows:(t + 1) * rows, :].astype(BF16)
        upper = rest[t * rows:t * rows + rows // 2, :]
        lower = rest[t * rows + rows // 2:(t + 1) * rows, :]
        out_ref[t, rows:rows + rows // 2, :] = jnp.where(left, upper, lower).astype(BF16)
        mixed = gather_lanes(sources, t, local)
        out_ref[t, rows + rows // 2:, :] = mixed.astype(BF16)
        sends[t].start()
    for copy in [both_copy] + sends:
        copy.wait()


def gather_lanes(sources, t, local):
    part, offset = (t * local) // LANES, (t * local) % LANES
    lane = iota((8, LANES), 1)
    mixed = jnp.zeros((8, LANES), F32)
    for i, source in enumerate(sources):
        piece = source[:, part * LANES:(part + 1) * LANES]
        shift = (i * local - offset) % LANES
        if shift:
            piece = pltpu.roll(piece, shift, 1)
        mixed = jnp.where((lane >= i * local) & (lane < (i + 1) * local), piece, mixed)
    return mixed


def weights_kernel(tables, rank, index_ref, x_ref, h_ref, both, keep_ref, give_ref):
    count, depth, width = x_ref.shape
    comp_width = h_ref.shape[2]
    local, comp_rows = width // tables, comp_width // tables
    x_all = x_ref[...].reshape(count * depth, width)
    h_all = h_ref[...].reshape(count * depth, comp_width)
    comp_grad = dot(h_all, x_all, 0, 0)
    proj_parts = dot(both[...], x_all, 0, 0)
    proj_grad = proj_parts[:rank] + proj_parts[rank:2 * rank]
    sources = [proj_grad[8 * i:8 * i + 8] for i in range(rank // 8)]
    even = (index_ref[0] % 2) == 0

    def weight_block(t):
        mine = comp_grad[t * comp_rows:(t + 1) * comp_rows]
        pieces = [mine[:, i * LANES:(i + 1) * LANES] for i in range(width // LANES)]
        return jnp.concatenate(pieces + [gather_lanes(sources, t, local)], axis=0)

    for i in range(tables // 2):
        zero, one = weight_block(2 * i), weight_block(2 * i + 1)
        keep_ref[i] = jnp.where(even, zero, one)
        give_ref[i] = jnp.where(even, one, zero)


def split(blocks, bits, index):
    if not bits:
        return [blocks]
    even = ((index >> bits[0]) % 2) == 0
    keep = [jnp.where(even, zero, one) for zero, one in zip(blocks[0::2], blocks[1::2])]
    give = [jnp.where(even, one, zero) for zero, one in zip(blocks[0::2], blocks[1::2])]
    return [part for pair in zip(split(keep, bits[1:], index), split(give, bits[1:], index)) for part in pair]


def total_of(refs, i):
    parts = [ref[i].astype(F32) for ref in refs]
    while len(parts) > 1:
        parts = [sum(parts[j:j + 2][1:], parts[j]) for j in range(0, len(parts), 2)]
    return parts[0]


def split_kernel(bits, index_ref, *refs):
    ins, outs = refs[:-2 ** len(bits)], refs[-2 ** len(bits):]
    parts = split([total_of(ins, i) for i in range(ins[0].shape[0])], bits, index_ref[0])
    for out, blocks in zip(outs, parts):
        for i, block in enumerate(blocks):
            out[i] = block.astype(out.dtype)


def add_kernel(*refs):
    refs[-1][0] = total_of(refs[:-1], 0)


def finish_kernel(scale, comp_rows, local, rank, after_ref, *refs):
    proj_ref, comp_ref = refs[-2:]
    total = total_of(refs[:-2], 0) * scale
    halves = comp_ref.shape[1] // LANES
    comp_ref[...] = jnp.concatenate([total[i * comp_rows:(i + 1) * comp_rows] for i in range(halves)], axis=1)
    mixed = total[halves * comp_rows:halves * comp_rows + 8].T
    proj_ref[...] = jnp.concatenate([mixed[i * local:(i + 1) * local, :] for i in range(rank // 8)], axis=1)


def hold_kernel(in_ref, out_ref):
    pass


def receive_kernel(block_rows, in_ref, counts_ref, rows_hbm, after_ref, rows_ref, sems):
    after_ref[...] = jnp.zeros_like(after_ref)
    copies = []
    tables = in_ref.shape[0]
    local, depth, slots = rows_ref.shape
    count = 8
    rows = local * count
    tail = rows + rows // 2
    mixed = in_ref[:, tail:, :].astype(F32)[:, :8, :]
    slot = 16.0 * mixed[:, :, 0:local] + mixed[:, :, local:2 * local]
    limits = (counts_ref[...] * block_rows).astype(F32)
    slot = jnp.where(slot < limits[None], slot, -1.0)
    target = iota((tables, count, 2 * slots), 2)
    targets = [target.astype(F32), jnp.where(target < slots, -2, target - slots).astype(F32)]
    half_pairs = max(local // 4, 1)
    for j in range(local // 2):
        hot = jnp.stack(
            [(slot[:, :, 2 * j + i:2 * j + i + 1] == targets[i]).astype(F32) for i in range(2)], axis=1
        ).reshape(tables * 2 * count, 2 * slots).astype(BF16)
        lead = in_ref[:, 16 * j:16 * j + 16, :].reshape(tables * 16, LANES)
        k = j % half_pairs
        other = in_ref[:, rows + 16 * k:rows + 16 * k + 16, :].reshape(tables * 16, LANES)
        top = dot(lead, hot, 0, 0).astype(BF16)
        bottom = dot(other, hot, 0, 0)
        at = HALF * (j // half_pairs)
        bottom = bottom[at:at + HALF].astype(BF16)
        for i in range(2):
            rows_ref[2 * j + i, 0:LANES, :] = top[:, i * slots:(i + 1) * slots]
            rows_ref[2 * j + i, LANES:, :] = bottom[:, i * slots:(i + 1) * slots]
        pair = pl.ds(2 * j, 2)
        copies.append(pltpu.make_async_copy(rows_ref.at[pair], rows_hbm.at[pair], sems.at[j]))
        copies[j].start()
    for copy in copies:
        copy.wait()


def shards(emb, grad_fm, grad_comp, proj, comp, slot, counts):
    count, width, depth = emb.shape
    rank = proj.shape[1]
    tables = lax.axis_size("table")
    groups = lax.axis_size("dp")
    local = width // tables
    slot_count = count * tables
    comp_width = comp.shape[0]
    comp_rows = comp_width // tables
    rows = local * count
    total_rows = rows + rows // 2 + 8
    vmem = pl.BlockSpec(memory_space=pltpu.VMEM)
    smem = pl.BlockSpec(memory_space=pltpu.SMEM)
    hbm = pl.BlockSpec(memory_space=pltpu.HBM)
    params = pltpu.CompilerParams(vmem_limit_bytes=40 * 1024 * 1024)
    large = pltpu.CompilerParams(vmem_limit_bytes=60 * 1024 * 1024)

    def call(body, name, outs, ins, specs, params=params, out=vmem, **more):
        return pl.pallas_call(
            body,
            out_shape=tuple(jax.ShapeDtypeStruct(*o) for o in outs),
            in_specs=specs,
            out_specs=out if isinstance(out, tuple) else (out,) * len(outs),
            compiler_params=params,
            name=name,
            **more,
        )(*ins)

    x, h = jnp.swapaxes(emb, 1, 2), jnp.swapaxes(grad_comp, 1, 2)
    index = lax.axis_index("table").astype(jnp.int32).reshape(1)
    part = comp_rows * (width // LANES) + 8
    shapes = [((tables, total_rows, LANES), BF16), ((count * depth, LANES), BF16)]
    sent, both = call(
        lambda *refs: send_kernel(tables, *refs),
        "send",
        shapes,
        (x, h, grad_fm, proj.T, comp, slot),
        [hbm] * 6,
        params=large,
        out=hbm,
        scratch_shapes=[
            pltpu.VMEM(x.shape, BF16),
            pltpu.VMEM(h.shape, BF16),
            pltpu.VMEM(grad_fm.shape, BF16),
            pltpu.VMEM((rank, width), BF16),
            pltpu.VMEM(comp.shape, BF16),
            pltpu.VMEM(slot.shape, jnp.int32),
            pltpu.VMEM((2, count * width // 2, 2 * LANES), BF16),
            pltpu.VMEM((count, width, LANES), BF16),
            pltpu.VMEM((count * depth, LANES), BF16),
            pltpu.VMEM((count, depth, LANES), BF16),
            pltpu.VMEM((count * width, LANES), F32),
            pltpu.VMEM((count * width, LANES), F32),
        ]
        + [pltpu.VMEM(*shapes[0])]
        + [pltpu.SemaphoreType.DMA((16 + tables,))],
    )
    def swap(array, offset, other_group=0):
        pairs = [
            (g * tables + i, (g ^ other_group) * tables + (i ^ offset)) for g in range(groups) for i in range(tables)
        ]
        return lax.ppermute(array, ("dp", "table"), pairs)

    bits = tables.bit_length() - 1
    got = lax.all_to_all(sent, "table", split_axis=0, concat_axis=0, tiled=True)
    keep, give = call(
        lambda *refs: weights_kernel(tables, rank, *refs),
        "weights",
        [((tables // 2, part, LANES), F32)] * 2,
        (index, x, h, both),
        [smem] + [vmem] * 3,
    )
    sums = [keep, swap(give, 1)]
    for stage in STAGES(bits):
        size = sums[0].shape[0] >> len(stage)
        cross = stage == STAGES(bits)[CROSS] and groups == 2
        kinds = [BF16 if cross else F32] + [BF16 if cross else LAST] * (2 ** len(stage) - 1)
        parts = call(
            lambda *refs, stage=stage: split_kernel(stage, *refs),
            "split",
            [((size, part, LANES), kind) for kind in kinds],
            (index, *sums),
            [smem] + [vmem] * len(sums),
            cost_estimate=pl.CostEstimate(flops=10**6, bytes_accessed=10**6, transcendentals=0),
        )
        sums = [p if o == 0 else swap(p, o << stage[0]) for o, p in enumerate(parts)]
        if cross:
            sums += [swap(p, o << stage[0], 1) for o, p in enumerate(parts)]
    step = 1
    while step < groups and groups != 2:
        keep, = call(add_kernel, "add", [(sums[0].shape, F32)], sums, [vmem] * len(sums))
        sums = [keep, swap(keep, 0, step)]
        step *= 2
    row_grads, after = call(
        lambda *refs: receive_kernel(slot_count // BLOCKS, *refs),
        "receive",
        [((local, depth, slot_count), BF16), ((8, LANES), F32)],
        (got, counts),
        [vmem] * 2,
        out=(hbm, vmem),
        scratch_shapes=[pltpu.VMEM((local, depth, slot_count), BF16), pltpu.SemaphoreType.DMA((local // 2,))],
    )
    scale = 1.0 / math.sqrt(count * tables * groups * depth)
    grad_proj, grad_comp_out = call(
        lambda *refs: finish_kernel(scale, comp_rows, local, rank, *refs),
        "finish",
        [((local, rank), F32), ((comp_rows, width), F32)],
        (after, *sums),
        [vmem] + [vmem] * len(sums),
    )
    return (jnp.swapaxes(row_grads, 1, 2)[None], grad_proj, grad_comp_out)


def solution(mesh):
    placed = (
        P(("dp", "table"), None, None),
        P(("dp", "table"), None),
        P(("dp", "table"), None, None),
        P(),
        P(),
        P(("dp", "table"), None),
        P("dp", "table"),
    )
    return jax.shard_map(
        shards,
        mesh=mesh,
        in_specs=placed,
        out_specs=(P("dp", "table", None, None), P("table", None), P("table", None)),
        check_vma=False,
    )
```

```python
import math

import jax
import jax.numpy as jnp
from jax import lax
from jax.experimental import pallas as pl
from jax.experimental.pallas import tpu as pltpu
from jax.sharding import PartitionSpec as P

BLOCKS = 4
F32 = jnp.float32
BF16 = jnp.bfloat16
LANES = 128
HALF = 64
CROSS = 0
LAST = BF16


def STAGES(bits):
    return [[b] for b in range(1, bits)]


def dot(a, b, ca, cb):
    return lax.dot_general(a, b, (((ca,), (cb,)), ((), ())), preferred_element_type=F32)


def iota(shape, dim):
    return lax.broadcasted_iota(jnp.int32, shape, dim)


def round_up(n, m):
    return -(-n // m) * m


def send_kernel(tables, x_hbm, h_hbm, g_hbm, proj_hbm, comp_hbm, slot_hbm, out_hbm, both_hbm,
                x_ref, h_ref, g_ref, proj_ref, comp_ref, slot_ref, spread, factors, both, swapped, main, rest, out_ref, sems):
    count, depth, width = x_ref.shape
    rank = proj_ref.shape[0]
    comp_width = comp_ref.shape[0]
    local, comp_rows = width // tables, comp_width // tables
    block = 8 * rank
    window = 2 * LANES

    pairs = [(g_hbm, g_ref), (proj_hbm, proj_ref), (comp_hbm, comp_ref), (slot_hbm, slot_ref)]
    small = [pltpu.make_async_copy(a, b, sems.at[i]) for i, (a, b) in enumerate(pairs)]
    pieces = 2
    size = count // pieces

    def in_pieces(a, b, at):
        parts = [pl.ds(p * size, size) for p in range(pieces)]
        return [pltpu.make_async_copy(a.at[p], b.at[p], sems.at[at + i]) for i, p in enumerate(parts)]

    x_copies = in_pieces(x_hbm, x_ref, 8 + tables)
    h_copies = in_pieces(h_hbm, h_ref, 8 + tables + pieces)
    for copy in small[:2] + x_copies + h_copies + small[2:]:
        copy.start()
    sends = [pltpu.make_async_copy(out_ref.at[t], out_hbm.at[t], sems.at[8 + t]) for t in range(tables)]
    both_copy = pltpu.make_async_copy(both, both_hbm, sems.at[6])

    row, col = iota((rank, LANES), 0), iota((rank, LANES), 1)
    eye = ((col == row) | (col == row + rank)).astype(F32)
    place = ((col == row + HALF) | (col == row + HALF + rank)).astype(BF16)
    sub, lane = iota((8, window), 0), iota((8, window), 1)
    folds, masks = [], []
    for start in (0, HALF):
        parts = [eye] * 8
        if start:
            parts = [jnp.zeros((start, LANES), F32)] + parts
        if window > start + block:
            parts = parts + [jnp.zeros((window - start - block, LANES), F32)]
        folds.append(jnp.concatenate(parts, axis=0).astype(BF16))
        masks.append((lane >= start + rank * sub) & (lane < start + rank * (sub + 1)))
    first = (iota((depth, LANES), 1) % HALF) < rank

    small[0].wait()
    small[1].wait()
    for a in range(width // 8):
        start, odd = (a * block) // LANES * LANES, a % 2
        piece = g_ref[:, start:start + window].astype(F32)
        for s in range(count):
            wide = jnp.broadcast_to(piece[s:s + 1, :], (8, window))
            spread[odd, s * (width // 2) + (a // 2) * 8:s * (width // 2) + (a // 2) * 8 + 8, :] = jnp.where(masks[odd], wide, 0.0).astype(BF16)
    placed_proj = dot(proj_ref[...], place, 0, 0)
    for s in range(count):
        lo, hi = s * (width // 2), (s + 1) * (width // 2)
        halves = [dot(spread[i, lo:hi, :], folds[i], 1, 0).reshape(width // 16, 8, LANES) for i in range(2)]
        columns = jnp.stack(halves, axis=1).reshape(width, LANES)
        factors[s] = (columns + placed_proj).astype(BF16)
    for copy in x_copies:
        copy.wait()
    for s in range(count):
        terms = dot(x_ref[s], factors[s], 1, 0)
        high = terms.astype(BF16).astype(F32)
        split = jnp.where(first, high, terms - high)
        both[s * depth:(s + 1) * depth, :] = split.astype(BF16)
        swapped[s] = pltpu.roll(split, HALF, 1).astype(BF16)
    for copy in h_copies:
        copy.wait()
    small[2].wait()
    small[3].wait()

    both_copy.start()

    comp_t = comp_ref[...].astype(F32).T.astype(BF16)
    slot = slot_ref[...]
    slot_high = slot // 16
    sources = [slot_high.astype(F32), (slot - 16 * slot_high).astype(F32)]
    rows = local * count
    left = iota((rows // 2, LANES), 1) < HALF
    span = width
    for part in range(1):
        begin, end = part * span, (part + 1) * span
        for s in range(count):
            h, other = h_ref[s], swapped[s]
            h_wide = jnp.concatenate([h, h[LANES:]], axis=0)
            other_wide = jnp.concatenate([other, other[LANES:]], axis=0)
            grads = dot(comp_t[begin:end], h_wide, 1, 1) + dot(factors[s, begin:end], other_wide, 1, 1)
            main[pl.ds(begin * count + s, span, stride=count), :] = grads[:, :LANES]
            rest[pl.ds(begin * count + s, span, stride=count), :] = grads[:, LANES:]
        for t in range(part * tables, (part + 1) * tables):
            out_ref[t, 0:rows, :] = main[t * rows:(t + 1) * rows, :].astype(BF16)
            upper = rest[t * rows:t * rows + rows // 2, :]
            lower = rest[t * rows + rows // 2:(t + 1) * rows, :]
            out_ref[t, rows:rows + rows // 2, :] = jnp.where(left, upper, lower).astype(BF16)
            out_ref[t, rows + rows // 2:, :] = gather_lanes(sources, t, local).astype(BF16)
            sends[t].start()
    for copy in [both_copy] + sends:
        copy.wait()


def gather_lanes(sources, t, local):
    part, offset = (t * local) // LANES, (t * local) % LANES
    lane = iota((8, LANES), 1)
    mixed = jnp.zeros((8, LANES), F32)
    for i, source in enumerate(sources):
        piece = source[:, part * LANES:(part + 1) * LANES]
        shift = (i * local - offset) % LANES
        if shift:
            piece = pltpu.roll(piece, shift, 1)
        mixed = jnp.where((lane >= i * local) & (lane < (i + 1) * local), piece, mixed)
    return mixed


def weights_kernel(tables, rank, index_ref, x_ref, h_ref, both, keep_ref, give_ref):
    count, depth, width = x_ref.shape
    comp_width = h_ref.shape[2]
    local, comp_rows = width // tables, comp_width // tables
    x_all = x_ref[...].reshape(count * depth, width)
    h_all = h_ref[...].reshape(count * depth, comp_width)
    comp_grad = dot(h_all, x_all, 0, 0)
    proj_parts = dot(both[...], x_all, 0, 0)
    proj_grad = proj_parts[:rank] + proj_parts[rank:2 * rank]
    sources = [proj_grad[8 * i:8 * i + 8] for i in range(rank // 8)]
    even = (index_ref[0] % 2) == 0

    def weight_block(t):
        mine = comp_grad[t * comp_rows:(t + 1) * comp_rows]
        pieces = [mine[:, i * LANES:(i + 1) * LANES] for i in range(width // LANES)]
        return jnp.concatenate(pieces + [gather_lanes(sources, t, local)], axis=0)

    for i in range(tables // 2):
        zero, one = weight_block(2 * i), weight_block(2 * i + 1)
        keep_ref[i] = jnp.where(even, zero, one)
        give_ref[i] = jnp.where(even, one, zero)


def split(blocks, bits, index):
    if not bits:
        return [blocks]
    even = ((index >> bits[0]) % 2) == 0
    keep = [jnp.where(even, zero, one) for zero, one in zip(blocks[0::2], blocks[1::2])]
    give = [jnp.where(even, one, zero) for zero, one in zip(blocks[0::2], blocks[1::2])]
    return [part for pair in zip(split(keep, bits[1:], index), split(give, bits[1:], index)) for part in pair]


def total_of(refs, i):
    parts = [ref[i].astype(F32) for ref in refs]
    while len(parts) > 1:
        parts = [sum(parts[j:j + 2][1:], parts[j]) for j in range(0, len(parts), 2)]
    return parts[0]


def split_kernel(bits, index_ref, *refs):
    ins, outs = refs[:-2 ** len(bits)], refs[-2 ** len(bits):]
    parts = split([total_of(ins, i) for i in range(ins[0].shape[0])], bits, index_ref[0])
    for out, blocks in zip(outs, parts):
        for i, block in enumerate(blocks):
            out[i] = block.astype(out.dtype)


def add_kernel(*refs):
    refs[-1][0] = total_of(refs[:-1], 0)


def finish_kernel(scale, comp_rows, local, rank, after_ref, *refs):
    proj_ref, comp_ref = refs[-2:]
    total = total_of(refs[:-2], 0) * scale
    halves = comp_ref.shape[1] // LANES
    comp_ref[...] = jnp.concatenate([total[i * comp_rows:(i + 1) * comp_rows] for i in range(halves)], axis=1)
    mixed = total[halves * comp_rows:halves * comp_rows + 8].T
    proj_ref[...] = jnp.concatenate([mixed[i * local:(i + 1) * local, :] for i in range(rank // 8)], axis=1)


def hold_kernel(in_ref, out_ref):
    pass


def receive_kernel(block_rows, in_ref, counts_ref, rows_hbm, after_ref, rows_ref, sems):
    after_ref[...] = jnp.zeros_like(after_ref)
    copies = []
    tables = in_ref.shape[0]
    local, depth, slots = rows_ref.shape
    count = 8
    rows = local * count
    tail = rows + rows // 2
    mixed = in_ref[:, tail:, :].astype(F32)[:, :8, :]
    slot = 16.0 * mixed[:, :, 0:local] + mixed[:, :, local:2 * local]
    limits = (counts_ref[...] * block_rows).astype(F32)
    slot = jnp.where(slot < limits[None], slot, -1.0)
    target = iota((tables, count, 2 * slots), 2)
    targets = [target.astype(F32), jnp.where(target < slots, -2, target - slots).astype(F32)]
    half_pairs = max(local // 4, 1)
    for j in range(local // 2):
        hot = jnp.stack(
            [(slot[:, :, 2 * j + i:2 * j + i + 1] == targets[i]).astype(F32) for i in range(2)], axis=1
        ).reshape(tables * 2 * count, 2 * slots).astype(BF16)
        lead = in_ref[:, 16 * j:16 * j + 16, :].reshape(tables * 16, LANES)
        k = j % half_pairs
        other = in_ref[:, rows + 16 * k:rows + 16 * k + 16, :].reshape(tables * 16, LANES)
        top = dot(lead, hot, 0, 0).astype(BF16)
        bottom = dot(other, hot, 0, 0)
        at = HALF * (j // half_pairs)
        bottom = bottom[at:at + HALF].astype(BF16)
        for i in range(2):
            rows_ref[2 * j + i, 0:LANES, :] = top[:, i * slots:(i + 1) * slots]
            rows_ref[2 * j + i, LANES:, :] = bottom[:, i * slots:(i + 1) * slots]
        pair = pl.ds(2 * j, 2)
        copies.append(pltpu.make_async_copy(rows_ref.at[pair], rows_hbm.at[pair], sems.at[j]))
        copies[j].start()
    for copy in copies:
        copy.wait()


def shards(emb, grad_fm, grad_comp, proj, comp, slot, counts):
    count, width, depth = emb.shape
    rank = proj.shape[1]
    tables = lax.axis_size("table")
    groups = lax.axis_size("dp")
    local = width // tables
    slot_count = count * tables
    comp_width = comp.shape[0]
    comp_rows = comp_width // tables
    rows = local * count
    total_rows = rows + rows // 2 + 8
    vmem = pl.BlockSpec(memory_space=pltpu.VMEM)
    smem = pl.BlockSpec(memory_space=pltpu.SMEM)
    hbm = pl.BlockSpec(memory_space=pltpu.HBM)
    params = pltpu.CompilerParams(vmem_limit_bytes=40 * 1024 * 1024)
    large = pltpu.CompilerParams(vmem_limit_bytes=60 * 1024 * 1024)

    def call(body, name, outs, ins, specs, params=params, out=vmem, **more):
        return pl.pallas_call(
            body,
            out_shape=tuple(jax.ShapeDtypeStruct(*o) for o in outs),
            in_specs=specs,
            out_specs=out if isinstance(out, tuple) else (out,) * len(outs),
            compiler_params=params,
            name=name,
            **more,
        )(*ins)

    x, h = jnp.swapaxes(emb, 1, 2), jnp.swapaxes(grad_comp, 1, 2)
    index = lax.axis_index("table").astype(jnp.int32).reshape(1)
    part = comp_rows * (width // LANES) + 8
    shapes = [((tables, total_rows, LANES), BF16), ((count * depth, LANES), BF16)]
    sent, both = call(
        lambda *refs: send_kernel(tables, *refs),
        "send",
        shapes,
        (x, h, grad_fm, proj.T, comp, slot),
        [hbm] * 6,
        params=large,
        out=hbm,
        scratch_shapes=[
            pltpu.VMEM(x.shape, BF16),
            pltpu.VMEM(h.shape, BF16),
            pltpu.VMEM(grad_fm.shape, BF16),
            pltpu.VMEM((rank, width), BF16),
            pltpu.VMEM(comp.shape, BF16),
            pltpu.VMEM(slot.shape, jnp.int32),
            pltpu.VMEM((2, count * width // 2, 2 * LANES), BF16),
            pltpu.VMEM((count, width, LANES), BF16),
            pltpu.VMEM((count * depth, LANES), BF16),
            pltpu.VMEM((count, depth, LANES), BF16),
            pltpu.VMEM((count * width, LANES), F32),
            pltpu.VMEM((count * width, LANES), F32),
        ]
        + [pltpu.VMEM(*shapes[0])]
        + [pltpu.SemaphoreType.DMA((16 + tables,))],
    )
    def swap(array, offset, other_group=0):
        pairs = [
            (g * tables + i, (g ^ other_group) * tables + (i ^ offset)) for g in range(groups) for i in range(tables)
        ]
        return lax.ppermute(array, ("dp", "table"), pairs)

    bits = tables.bit_length() - 1
    got = lax.all_to_all(sent, "table", split_axis=0, concat_axis=0, tiled=True)
    keep, give = call(
        lambda *refs: weights_kernel(tables, rank, *refs),
        "weights",
        [((tables // 2, part, LANES), F32)] * 2,
        (index, x, h, both),
        [smem] + [vmem] * 3,
    )
    sums = [keep, swap(give, 1)]
    for stage in STAGES(bits):
        size = sums[0].shape[0] >> len(stage)
        cross = stage == STAGES(bits)[CROSS] and groups == 2
        kinds = [BF16 if cross else F32] + [BF16 if cross else LAST] * (2 ** len(stage) - 1)
        parts = call(
            lambda *refs, stage=stage: split_kernel(stage, *refs),
            "split",
            [((size, part, LANES), kind) for kind in kinds],
            (index, *sums),
            [smem] + [vmem] * len(sums),
            cost_estimate=pl.CostEstimate(flops=10**6, bytes_accessed=10**6, transcendentals=0),
        )
        sums = [p if o == 0 else swap(p, o << stage[0]) for o, p in enumerate(parts)]
        if cross:
            sums += [swap(p, o << stage[0], 1) for o, p in enumerate(parts)]
    step = 1
    while step < groups and groups != 2:
        keep, = call(add_kernel, "add", [(sums[0].shape, F32)], sums, [vmem] * len(sums))
        sums = [keep, swap(keep, 0, step)]
        step *= 2
    row_grads, after = call(
        lambda *refs: receive_kernel(slot_count // BLOCKS, *refs),
        "receive",
        [((local, depth, slot_count), BF16), ((8, LANES), F32)],
        (got, counts),
        [vmem] * 2,
        out=(hbm, vmem),
        scratch_shapes=[pltpu.VMEM((local, depth, slot_count), BF16), pltpu.SemaphoreType.DMA((local // 2,))],
    )
    scale = 1.0 / math.sqrt(count * tables * groups * depth)
    grad_proj, grad_comp_out = call(
        lambda *refs: finish_kernel(scale, comp_rows, local, rank, *refs),
        "finish",
        [((local, rank), F32), ((comp_rows, width), F32)],
        (after, *sums),
        [vmem] + [vmem] * len(sums),
    )
    return (jnp.swapaxes(row_grads, 1, 2)[None], grad_proj, grad_comp_out)


def solution(mesh):
    placed = (
        P(("dp", "table"), None, None),
        P(("dp", "table"), None),
        P(("dp", "table"), None, None),
        P(),
        P(),
        P(("dp", "table"), None),
        P("dp", "table"),
    )
    return jax.shard_map(
        shards,
        mesh=mesh,
        in_specs=placed,
        out_specs=(P("dp", "table", None, None), P("table", None), P("table", None)),
        check_vma=False,
    )
```

```python
import math

import jax
import jax.numpy as jnp
from jax import lax
from jax.experimental import pallas as pl
from jax.experimental.pallas import tpu as pltpu
from jax.sharding import PartitionSpec as P

BLOCKS = 4
F32 = jnp.float32
BF16 = jnp.bfloat16
LANES = 128
HALF = 64
CROSS = 1
LAST = F32


def STAGES(bits):
    return [[b] for b in range(bits - 1)]


def dot(a, b, ca, cb):
    return lax.dot_general(a, b, (((ca,), (cb,)), ((), ())), preferred_element_type=F32)


def iota(shape, dim):
    return lax.broadcasted_iota(jnp.int32, shape, dim)


def round_up(n, m):
    return -(-n // m) * m


def send_kernel(tables, index_ref, x_hbm, h_hbm, g_hbm, proj_hbm, comp_hbm, slot_hbm, out_hbm, keep_hbm, give_hbm,
                x_ref, h_ref, g_ref, proj_ref, comp_ref, slot_ref, spread, factors, both, swapped, main, rest, out_ref, keep_ref, give_ref, sems):
    count, depth, width = x_ref.shape
    rank = proj_ref.shape[0]
    comp_width = comp_ref.shape[0]
    local, comp_rows = width // tables, comp_width // tables
    block = 8 * rank
    window = 2 * LANES

    pairs = [(g_hbm, g_ref), (proj_hbm, proj_ref), (comp_hbm, comp_ref), (slot_hbm, slot_ref)]
    small = [pltpu.make_async_copy(a, b, sems.at[i]) for i, (a, b) in enumerate(pairs)]
    pieces = 2
    size = count // pieces

    def in_pieces(a, b, at):
        parts = [pl.ds(p * size, size) for p in range(pieces)]
        return [pltpu.make_async_copy(a.at[p], b.at[p], sems.at[at + i]) for i, p in enumerate(parts)]

    x_copies = in_pieces(x_hbm, x_ref, 8 + tables)
    h_copies = in_pieces(h_hbm, h_ref, 8 + tables + pieces)
    for copy in small[:2] + x_copies + h_copies + small[2:]:
        copy.start()
    sends = [pltpu.make_async_copy(out_ref.at[t], out_hbm.at[t], sems.at[8 + t]) for t in range(tables)]
    part_copies = [
        pltpu.make_async_copy(give_ref, give_hbm, sems.at[6]), pltpu.make_async_copy(keep_ref, keep_hbm, sems.at[7])
    ]

    row, col = iota((rank, LANES), 0), iota((rank, LANES), 1)
    eye = ((col == row) | (col == row + rank)).astype(F32)
    place = ((col == row + HALF) | (col == row + HALF + rank)).astype(BF16)
    sub, lane = iota((8, window), 0), iota((8, window), 1)
    folds, masks = [], []
    for start in (0, HALF):
        parts = [eye] * 8
        if start:
            parts = [jnp.zeros((start, LANES), F32)] + parts
        if window > start + block:
            parts = parts + [jnp.zeros((window - start - block, LANES), F32)]
        folds.append(jnp.concatenate(parts, axis=0).astype(BF16))
        masks.append((lane >= start + rank * sub) & (lane < start + rank * (sub + 1)))
    first = (iota((depth, LANES), 1) % HALF) < rank

    small[0].wait()
    small[1].wait()
    for a in range(width // 8):
        start, odd = (a * block) // LANES * LANES, a % 2
        piece = g_ref[:, start:start + window].astype(F32)
        for s in range(count):
            wide = jnp.broadcast_to(piece[s:s + 1, :], (8, window))
            spread[odd, s * (width // 2) + (a // 2) * 8:s * (width // 2) + (a // 2) * 8 + 8, :] = jnp.where(masks[odd], wide, 0.0).astype(BF16)
    placed_proj = dot(proj_ref[...], place, 0, 0)
    for s in range(count):
        lo, hi = s * (width // 2), (s + 1) * (width // 2)
        halves = [dot(spread[i, lo:hi, :], folds[i], 1, 0).reshape(width // 16, 8, LANES) for i in range(2)]
        columns = jnp.stack(halves, axis=1).reshape(width, LANES)
        factors[s] = (columns + placed_proj).astype(BF16)
    for copy in x_copies:
        copy.wait()
    for s in range(count):
        terms = dot(x_ref[s], factors[s], 1, 0)
        high = terms.astype(BF16).astype(F32)
        split = jnp.where(first, high, terms - high)
        both[s * depth:(s + 1) * depth, :] = split.astype(BF16)
        swapped[s] = pltpu.roll(split, HALF, 1).astype(BF16)
    for copy in h_copies:
        copy.wait()
    small[2].wait()
    small[3].wait()

    blocks = weight_blocks(tables, rank, x_ref, h_ref, both)
    low = index_ref[0] < tables // 2
    for i in range(tables // 2):
        near, far = blocks[i], blocks[i + tables // 2]
        keep_ref[i] = jnp.where(low, near, far)
        give_ref[i] = jnp.where(low, far, near).astype(BF16)
    for copy in part_copies:
        copy.start()

    comp_t = comp_ref[...].astype(F32).T.astype(BF16)
    slot = slot_ref[...]
    slot_high = slot // 16
    sources = [slot_high.astype(F32), (slot - 16 * slot_high).astype(F32)]
    rows = local * count
    left = iota((rows // 2, LANES), 1) < HALF
    span = width
    for part in range(1):
        begin, end = part * span, (part + 1) * span
        for s in range(count):
            h, other = h_ref[s], swapped[s]
            h_wide = jnp.concatenate([h, h[LANES:]], axis=0)
            other_wide = jnp.concatenate([other, other[LANES:]], axis=0)
            grads = dot(comp_t[begin:end], h_wide, 1, 1) + dot(factors[s, begin:end], other_wide, 1, 1)
            main[pl.ds(begin * count + s, span, stride=count), :] = grads[:, :LANES]
            rest[pl.ds(begin * count + s, span, stride=count), :] = grads[:, LANES:]
        for t in range(part * tables, (part + 1) * tables):
            out_ref[t, 0:rows, :] = main[t * rows:(t + 1) * rows, :].astype(BF16)
            upper = rest[t * rows:t * rows + rows // 2, :]
            lower = rest[t * rows + rows // 2:(t + 1) * rows, :]
            out_ref[t, rows:rows + rows // 2, :] = jnp.where(left, upper, lower).astype(BF16)
            out_ref[t, rows + rows // 2:, :] = gather_lanes(sources, t, local).astype(BF16)
            sends[t].start()
    for copy in part_copies + sends:
        copy.wait()


def gather_lanes(sources, t, local):
    part, offset = (t * local) // LANES, (t * local) % LANES
    lane = iota((8, LANES), 1)
    mixed = jnp.zeros((8, LANES), F32)
    for i, source in enumerate(sources):
        piece = source[:, part * LANES:(part + 1) * LANES]
        shift = (i * local - offset) % LANES
        if shift:
            piece = pltpu.roll(piece, shift, 1)
        mixed = jnp.where((lane >= i * local) & (lane < (i + 1) * local), piece, mixed)
    return mixed


def weight_blocks(tables, rank, x_ref, h_ref, both):
    count, depth, width = x_ref.shape
    comp_width = h_ref.shape[2]
    local, comp_rows = width // tables, comp_width // tables
    x_all = x_ref[...].reshape(count * depth, width)
    h_all = h_ref[...].reshape(count * depth, comp_width)
    comp_grad = dot(h_all, x_all, 0, 0)
    proj_parts = dot(both[...], x_all, 0, 0)
    proj_grad = proj_parts[:rank] + proj_parts[rank:2 * rank]
    sources = [proj_grad[8 * i:8 * i + 8] for i in range(rank // 8)]

    def weight_block(t):
        mine = comp_grad[t * comp_rows:(t + 1) * comp_rows]
        pieces = [mine[:, i * LANES:(i + 1) * LANES] for i in range(width // LANES)]
        return jnp.concatenate(pieces + [gather_lanes(sources, t, local)], axis=0)

    return [weight_block(t) for t in range(tables)]


def split(blocks, bits, index):
    if not bits:
        return [blocks]
    even = ((index >> bits[0]) % 2) == 0
    keep = [jnp.where(even, zero, one) for zero, one in zip(blocks[0::2], blocks[1::2])]
    give = [jnp.where(even, one, zero) for zero, one in zip(blocks[0::2], blocks[1::2])]
    return [part for pair in zip(split(keep, bits[1:], index), split(give, bits[1:], index)) for part in pair]


def total_of(refs, i):
    parts = [ref[i].astype(F32) for ref in refs]
    while len(parts) > 1:
        parts = [sum(parts[j:j + 2][1:], parts[j]) for j in range(0, len(parts), 2)]
    return parts[0]


def split_kernel(bits, index_ref, *refs):
    ins, outs = refs[:-2 ** len(bits)], refs[-2 ** len(bits):]
    parts = split([total_of(ins, i) for i in range(ins[0].shape[0])], bits, index_ref[0])
    for out, blocks in zip(outs, parts):
        for i, block in enumerate(blocks):
            out[i] = block.astype(out.dtype)


def add_kernel(*refs):
    refs[-1][0] = total_of(refs[:-1], 0)


def write_weights(scale, comp_rows, local, rank, refs, proj_ref, comp_ref):
    total = total_of(refs, 0) * scale
    halves = comp_ref.shape[1] // LANES
    comp_ref[...] = jnp.concatenate([total[i * comp_rows:(i + 1) * comp_rows] for i in range(halves)], axis=1)
    mixed = total[halves * comp_rows:halves * comp_rows + 8].T
    proj_ref[...] = jnp.concatenate([mixed[i * local:(i + 1) * local, :] for i in range(rank // 8)], axis=1)


def hold_kernel(in_ref, out_ref):
    pass


def receive_kernel(block_rows, scale, rank, in_ref, counts_ref, *refs):
    sums, (rows_hbm, proj_hbm, comp_hbm, rows_ref, proj_ref, comp_ref, sems) = refs[:-7], refs[-7:]
    write_weights(scale, comp_ref.shape[0], rows_ref.shape[0], rank, sums, proj_ref, comp_ref)
    pairs = rows_ref.shape[0] // 2
    weights = [
        pltpu.make_async_copy(proj_ref, proj_hbm, sems.at[pairs]),
        pltpu.make_async_copy(comp_ref, comp_hbm, sems.at[pairs + 1]),
    ]
    for copy in weights:
        copy.start()
    copies = []
    tables = in_ref.shape[0]
    local, depth, slots = rows_ref.shape
    count = 8
    rows = local * count
    tail = rows + rows // 2
    mixed = in_ref[:, tail:, :].astype(F32)[:, :8, :]
    slot = 16.0 * mixed[:, :, 0:local] + mixed[:, :, local:2 * local]
    limits = (counts_ref[...] * block_rows).astype(F32)
    slot = jnp.where(slot < limits[None], slot, -1.0)
    target = iota((tables, count, 2 * slots), 2)
    targets = [target.astype(F32), jnp.where(target < slots, -2, target - slots).astype(F32)]
    half_pairs = max(local // 4, 1)
    for j in range(local // 2):
        hot = jnp.stack(
            [(slot[:, :, 2 * j + i:2 * j + i + 1] == targets[i]).astype(F32) for i in range(2)], axis=1
        ).reshape(tables * 2 * count, 2 * slots).astype(BF16)
        lead = in_ref[:, 16 * j:16 * j + 16, :].reshape(tables * 16, LANES)
        k = j % half_pairs
        other = in_ref[:, rows + 16 * k:rows + 16 * k + 16, :].reshape(tables * 16, LANES)
        top = dot(lead, hot, 0, 0).astype(BF16)
        bottom = dot(other, hot, 0, 0)
        at = HALF * (j // half_pairs)
        bottom = bottom[at:at + HALF].astype(BF16)
        for i in range(2):
            rows_ref[2 * j + i, 0:LANES, :] = top[:, i * slots:(i + 1) * slots]
            rows_ref[2 * j + i, LANES:, :] = bottom[:, i * slots:(i + 1) * slots]
        pair = pl.ds(2 * j, 2)
        copies.append(pltpu.make_async_copy(rows_ref.at[pair], rows_hbm.at[pair], sems.at[j]))
        copies[j].start()
    for copy in copies + weights:
        copy.wait()


def shards(emb, grad_fm, grad_comp, proj, comp, slot, counts):
    count, width, depth = emb.shape
    rank = proj.shape[1]
    tables = lax.axis_size("table")
    groups = lax.axis_size("dp")
    local = width // tables
    slot_count = count * tables
    comp_width = comp.shape[0]
    comp_rows = comp_width // tables
    rows = local * count
    total_rows = rows + rows // 2 + 8
    vmem = pl.BlockSpec(memory_space=pltpu.VMEM)
    smem = pl.BlockSpec(memory_space=pltpu.SMEM)
    hbm = pl.BlockSpec(memory_space=pltpu.HBM)
    params = pltpu.CompilerParams(vmem_limit_bytes=40 * 1024 * 1024)
    large = pltpu.CompilerParams(vmem_limit_bytes=60 * 1024 * 1024)

    def call(body, name, outs, ins, specs, params=params, out=vmem, **more):
        return pl.pallas_call(
            body,
            out_shape=tuple(jax.ShapeDtypeStruct(*o) for o in outs),
            in_specs=specs,
            out_specs=out if isinstance(out, tuple) else (out,) * len(outs),
            compiler_params=params,
            name=name,
            **more,
        )(*ins)

    x, h = jnp.swapaxes(emb, 1, 2), jnp.swapaxes(grad_comp, 1, 2)
    index = lax.axis_index("table").astype(jnp.int32).reshape(1)
    part = comp_rows * (width // LANES) + 8
    shapes = [
        ((tables, total_rows, LANES), BF16), ((tables // 2, part, LANES), F32), ((tables // 2, part, LANES), BF16)
    ]
    sent, keep, give = call(
        lambda *refs: send_kernel(tables, *refs),
        "send",
        shapes,
        (index, x, h, grad_fm, proj.T, comp, slot),
        [smem] + [hbm] * 6,
        params=large,
        out=hbm,
        scratch_shapes=[
            pltpu.VMEM(x.shape, BF16),
            pltpu.VMEM(h.shape, BF16),
            pltpu.VMEM(grad_fm.shape, BF16),
            pltpu.VMEM((rank, width), BF16),
            pltpu.VMEM(comp.shape, BF16),
            pltpu.VMEM(slot.shape, jnp.int32),
            pltpu.VMEM((2, count * width // 2, 2 * LANES), BF16),
            pltpu.VMEM((count, width, LANES), BF16),
            pltpu.VMEM((count * depth, LANES), BF16),
            pltpu.VMEM((count, depth, LANES), BF16),
            pltpu.VMEM((count * width, LANES), F32),
            pltpu.VMEM((count * width, LANES), F32),
        ]
        + [pltpu.VMEM(*o) for o in shapes]
        + [pltpu.SemaphoreType.DMA((16 + tables,))],
    )
    def swap(array, offset, other_group=0):
        pairs = [
            (g * tables + i, (g ^ other_group) * tables + (i ^ offset)) for g in range(groups) for i in range(tables)
        ]
        return lax.ppermute(array, ("dp", "table"), pairs)

    bits = tables.bit_length() - 1
    sums = [keep, swap(give, tables // 2)]
    got = lax.all_to_all(sent, "table", split_axis=0, concat_axis=0, tiled=True)
    for stage in STAGES(bits):
        size = sums[0].shape[0] >> len(stage)
        cross = stage == STAGES(bits)[CROSS] and groups == 2
        kinds = [F32] + [LAST] * (2 ** len(stage) - 1)
        parts = call(
            lambda *refs, stage=stage: split_kernel(stage, *refs),
            "split",
            [((size, part, LANES), kind) for kind in kinds],
            (index, *sums),
            [smem] + [vmem] * len(sums),
            cost_estimate=pl.CostEstimate(flops=10**11 if stage == STAGES(bits)[0] else 10**6, bytes_accessed=10**6, transcendentals=0),
        )
        sums = [p if o == 0 else swap(p, o << stage[0]) for o, p in enumerate(parts)]
        if cross:
            sums += [swap(p, o << stage[0], 1) for o, p in enumerate(parts)]
    step = 1
    while step < groups and groups != 2:
        keep, = call(add_kernel, "add", [(sums[0].shape, F32)], sums, [vmem] * len(sums))
        sums = [keep, swap(keep, 0, step)]
        step *= 2
    scale = 1.0 / math.sqrt(count * tables * groups * depth)
    row_grads, grad_proj, grad_comp_out = call(
        lambda *refs: receive_kernel(slot_count // BLOCKS, scale, rank, *refs),
        "receive",
        [((local, depth, slot_count), BF16), ((local, rank), F32), ((comp_rows, width), F32)],
        (got, counts, *sums),
        [vmem] * (2 + len(sums)),
        out=hbm,
        scratch_shapes=[
            pltpu.VMEM((local, depth, slot_count), BF16),
            pltpu.VMEM((local, rank), F32),
            pltpu.VMEM((comp_rows, width), F32),
            pltpu.SemaphoreType.DMA((local // 2 + 2,)),
        ],
    )
    return (jnp.swapaxes(row_grads, 1, 2)[None], grad_proj, grad_comp_out)


def solution(mesh):
    placed = (
        P(("dp", "table"), None, None),
        P(("dp", "table"), None),
        P(("dp", "table"), None, None),
        P(),
        P(),
        P(("dp", "table"), None),
        P("dp", "table"),
    )
    return jax.shard_map(
        shards,
        mesh=mesh,
        in_specs=placed,
        out_specs=(P("dp", "table", None, None), P("table", None), P("table", None)),
        check_vma=False,
    )
```

```python
import math

import jax
import jax.numpy as jnp
from jax import lax
from jax.experimental import pallas as pl
from jax.experimental.pallas import tpu as pltpu
from jax.sharding import PartitionSpec as P

BLOCKS = 4
F32 = jnp.float32
BF16 = jnp.bfloat16
LANES = 128
HALF = 64
CROSS = 1
LAST = F32


def STAGES(bits):
    return [[b] for b in range(bits - 1)]


def dot(a, b, ca, cb):
    return lax.dot_general(a, b, (((ca,), (cb,)), ((), ())), preferred_element_type=F32)


def iota(shape, dim):
    return lax.broadcasted_iota(jnp.int32, shape, dim)


def round_up(n, m):
    return -(-n // m) * m


def send_kernel(tables, index_ref, x_hbm, h_hbm, g_hbm, proj_hbm, comp_hbm, slot_hbm, out_hbm, both_hbm, give_hbm,
                x_ref, h_ref, g_ref, proj_ref, comp_ref, slot_ref, spread, factors, both, swapped, main, rest, out_ref, give_ref, sems):
    count, depth, width = x_ref.shape
    rank = proj_ref.shape[0]
    comp_width = comp_ref.shape[0]
    local, comp_rows = width // tables, comp_width // tables
    block = 8 * rank
    window = 2 * LANES

    pairs = [(g_hbm, g_ref), (proj_hbm, proj_ref), (comp_hbm, comp_ref), (slot_hbm, slot_ref)]
    small = [pltpu.make_async_copy(a, b, sems.at[i]) for i, (a, b) in enumerate(pairs)]
    pieces = 2
    size = count // pieces

    def in_pieces(a, b, at):
        parts = [pl.ds(p * size, size) for p in range(pieces)]
        return [pltpu.make_async_copy(a.at[p], b.at[p], sems.at[at + i]) for i, p in enumerate(parts)]

    x_copies = in_pieces(x_hbm, x_ref, 8 + tables)
    h_copies = in_pieces(h_hbm, h_ref, 8 + tables + pieces)
    for copy in small[:2] + x_copies + h_copies + small[2:]:
        copy.start()
    sends = [pltpu.make_async_copy(out_ref.at[t], out_hbm.at[t], sems.at[8 + t]) for t in range(tables)]
    part_copies = [
        pltpu.make_async_copy(give_ref, give_hbm, sems.at[6]), pltpu.make_async_copy(both, both_hbm, sems.at[7])
    ]

    row, col = iota((rank, LANES), 0), iota((rank, LANES), 1)
    eye = ((col == row) | (col == row + rank)).astype(F32)
    place = ((col == row + HALF) | (col == row + HALF + rank)).astype(BF16)
    sub, lane = iota((8, window), 0), iota((8, window), 1)
    folds, masks = [], []
    for start in (0, HALF):
        parts = [eye] * 8
        if start:
            parts = [jnp.zeros((start, LANES), F32)] + parts
        if window > start + block:
            parts = parts + [jnp.zeros((window - start - block, LANES), F32)]
        folds.append(jnp.concatenate(parts, axis=0).astype(BF16))
        masks.append((lane >= start + rank * sub) & (lane < start + rank * (sub + 1)))
    first = (iota((depth, LANES), 1) % HALF) < rank

    small[0].wait()
    small[1].wait()
    for a in range(width // 8):
        start, odd = (a * block) // LANES * LANES, a % 2
        piece = g_ref[:, start:start + window].astype(F32)
        for s in range(count):
            wide = jnp.broadcast_to(piece[s:s + 1, :], (8, window))
            spread[odd, s * (width // 2) + (a // 2) * 8:s * (width // 2) + (a // 2) * 8 + 8, :] = jnp.where(masks[odd], wide, 0.0).astype(BF16)
    placed_proj = dot(proj_ref[...], place, 0, 0)
    for s in range(count):
        lo, hi = s * (width // 2), (s + 1) * (width // 2)
        halves = [dot(spread[i, lo:hi, :], folds[i], 1, 0).reshape(width // 16, 8, LANES) for i in range(2)]
        columns = jnp.stack(halves, axis=1).reshape(width, LANES)
        factors[s] = (columns + placed_proj).astype(BF16)
    for copy in x_copies:
        copy.wait()
    for s in range(count):
        terms = dot(x_ref[s], factors[s], 1, 0)
        high = terms.astype(BF16).astype(F32)
        split = jnp.where(first, high, terms - high)
        both[s * depth:(s + 1) * depth, :] = split.astype(BF16)
        swapped[s] = pltpu.roll(split, HALF, 1).astype(BF16)
    for copy in h_copies:
        copy.wait()
    small[2].wait()
    small[3].wait()

    half = 1 - index_ref[0] // (tables // 2)
    for i, block in enumerate(half_blocks(tables, rank, x_ref, h_ref, both, half)):
        give_ref[i] = block.astype(BF16)
    for copy in part_copies:
        copy.start()

    comp_t = comp_ref[...].astype(F32).T.astype(BF16)
    slot = slot_ref[...]
    slot_high = slot // 16
    sources = [slot_high.astype(F32), (slot - 16 * slot_high).astype(F32)]
    rows = local * count
    left = iota((rows // 2, LANES), 1) < HALF
    span = width
    for part in range(1):
        begin, end = part * span, (part + 1) * span
        for s in range(count):
            h, other = h_ref[s], swapped[s]
            h_wide = jnp.concatenate([h, h[LANES:]], axis=0)
            other_wide = jnp.concatenate([other, other[LANES:]], axis=0)
            grads = dot(comp_t[begin:end], h_wide, 1, 1) + dot(factors[s, begin:end], other_wide, 1, 1)
            main[pl.ds(begin * count + s, span, stride=count), :] = grads[:, :LANES]
            rest[pl.ds(begin * count + s, span, stride=count), :] = grads[:, LANES:]
        for t in range(part * tables, (part + 1) * tables):
            out_ref[t, 0:rows, :] = main[t * rows:(t + 1) * rows, :].astype(BF16)
            upper = rest[t * rows:t * rows + rows // 2, :]
            lower = rest[t * rows + rows // 2:(t + 1) * rows, :]
            out_ref[t, rows:rows + rows // 2, :] = jnp.where(left, upper, lower).astype(BF16)
            out_ref[t, rows + rows // 2:, :] = gather_lanes(sources, t, local).astype(BF16)
            sends[t].start()
    for copy in part_copies + sends:
        copy.wait()


def gather_lanes(sources, t, local):
    part, offset = (t * local) // LANES, (t * local) % LANES
    lane = iota((8, LANES), 1)
    mixed = jnp.zeros((8, LANES), F32)
    for i, source in enumerate(sources):
        piece = source[:, part * LANES:(part + 1) * LANES]
        shift = (i * local - offset) % LANES
        if shift:
            piece = pltpu.roll(piece, shift, 1)
        mixed = jnp.where((lane >= i * local) & (lane < (i + 1) * local), piece, mixed)
    return mixed


def half_blocks(tables, rank, x_ref, h_ref, both, half):
    count, depth, width = x_ref.shape
    comp_width = h_ref.shape[2]
    local, comp_rows = width // tables, comp_width // tables
    h_lanes = pl.ds(pl.multiple_of(half * (comp_width // 2), LANES), comp_width // 2)
    x_lanes = pl.ds(pl.multiple_of(half * (width // 2), LANES), width // 2)
    x_all = x_ref[...].reshape(count * depth, width)
    h_half = h_ref[:, :, h_lanes].reshape(count * depth, comp_width // 2)
    x_half = x_ref[:, :, x_lanes].reshape(count * depth, width // 2)
    comp_grad = dot(h_half, x_all, 0, 0)
    proj_parts = dot(both[...], x_half, 0, 0)
    proj_grad = proj_parts[:rank] + proj_parts[rank:2 * rank]
    sources = [proj_grad[8 * i:8 * i + 8] for i in range(rank // 8)]

    def block(t):
        mine = comp_grad[t * comp_rows:(t + 1) * comp_rows]
        pieces = [mine[:, i * LANES:(i + 1) * LANES] for i in range(width // LANES)]
        return jnp.concatenate(pieces + [gather_lanes(sources, t, local)], axis=0)

    return [block(t) for t in range(tables // 2)]


def keep_kernel(tables, rank, index_ref, x_ref, h_ref, both, keep_ref):
    half = index_ref[0] // (tables // 2)
    for i, block in enumerate(half_blocks(tables, rank, x_ref, h_ref, both, half)):
        keep_ref[i] = block


def split(blocks, bits, index):
    if not bits:
        return [blocks]
    even = ((index >> bits[0]) % 2) == 0
    keep = [jnp.where(even, zero, one) for zero, one in zip(blocks[0::2], blocks[1::2])]
    give = [jnp.where(even, one, zero) for zero, one in zip(blocks[0::2], blocks[1::2])]
    return [part for pair in zip(split(keep, bits[1:], index), split(give, bits[1:], index)) for part in pair]


def total_of(refs, i):
    parts = [ref[i].astype(F32) for ref in refs]
    while len(parts) > 1:
        parts = [sum(parts[j:j + 2][1:], parts[j]) for j in range(0, len(parts), 2)]
    return parts[0]


def split_kernel(bits, index_ref, *refs):
    ins, outs = refs[:-2 ** len(bits)], refs[-2 ** len(bits):]
    parts = split([total_of(ins, i) for i in range(ins[0].shape[0])], bits, index_ref[0])
    for out, blocks in zip(outs, parts):
        for i, block in enumerate(blocks):
            out[i] = block.astype(out.dtype)


def add_kernel(*refs):
    refs[-1][0] = total_of(refs[:-1], 0)


def write_weights(scale, comp_rows, local, rank, refs, proj_ref, comp_ref):
    total = total_of(refs, 0) * scale
    halves = comp_ref.shape[1] // LANES
    comp_ref[...] = jnp.concatenate([total[i * comp_rows:(i + 1) * comp_rows] for i in range(halves)], axis=1)
    mixed = total[halves * comp_rows:halves * comp_rows + 8].T
    proj_ref[...] = jnp.concatenate([mixed[i * local:(i + 1) * local, :] for i in range(rank // 8)], axis=1)


def hold_kernel(in_ref, out_ref):
    pass


def receive_kernel(block_rows, scale, rank, in_ref, counts_ref, *refs):
    sums, (rows_hbm, proj_hbm, comp_hbm, rows_ref, proj_ref, comp_ref, sems) = refs[:-7], refs[-7:]
    write_weights(scale, comp_ref.shape[0], rows_ref.shape[0], rank, sums, proj_ref, comp_ref)
    pairs = rows_ref.shape[0] // 2
    weights = [
        pltpu.make_async_copy(proj_ref, proj_hbm, sems.at[pairs]),
        pltpu.make_async_copy(comp_ref, comp_hbm, sems.at[pairs + 1]),
    ]
    for copy in weights:
        copy.start()
    copies = []
    tables = in_ref.shape[0]
    local, depth, slots = rows_ref.shape
    count = 8
    rows = local * count
    tail = rows + rows // 2
    mixed = in_ref[:, tail:, :].astype(F32)[:, :8, :]
    slot = 16.0 * mixed[:, :, 0:local] + mixed[:, :, local:2 * local]
    limits = (counts_ref[...] * block_rows).astype(F32)
    slot = jnp.where(slot < limits[None], slot, -1.0)
    target = iota((tables, count, 2 * slots), 2)
    targets = [target.astype(F32), jnp.where(target < slots, -2, target - slots).astype(F32)]
    half_pairs = max(local // 4, 1)
    for j in range(local // 2):
        hot = jnp.stack(
            [(slot[:, :, 2 * j + i:2 * j + i + 1] == targets[i]).astype(F32) for i in range(2)], axis=1
        ).reshape(tables * 2 * count, 2 * slots).astype(BF16)
        lead = in_ref[:, 16 * j:16 * j + 16, :].reshape(tables * 16, LANES)
        k = j % half_pairs
        other = in_ref[:, rows + 16 * k:rows + 16 * k + 16, :].reshape(tables * 16, LANES)
        top = dot(lead, hot, 0, 0).astype(BF16)
        bottom = dot(other, hot, 0, 0)
        at = HALF * (j // half_pairs)
        bottom = bottom[at:at + HALF].astype(BF16)
        for i in range(2):
            rows_ref[2 * j + i, 0:LANES, :] = top[:, i * slots:(i + 1) * slots]
            rows_ref[2 * j + i, LANES:, :] = bottom[:, i * slots:(i + 1) * slots]
        pair = pl.ds(2 * j, 2)
        copies.append(pltpu.make_async_copy(rows_ref.at[pair], rows_hbm.at[pair], sems.at[j]))
        copies[j].start()
    for copy in copies + weights:
        copy.wait()


def shards(emb, grad_fm, grad_comp, proj, comp, slot, counts):
    count, width, depth = emb.shape
    rank = proj.shape[1]
    tables = lax.axis_size("table")
    groups = lax.axis_size("dp")
    local = width // tables
    slot_count = count * tables
    comp_width = comp.shape[0]
    comp_rows = comp_width // tables
    rows = local * count
    total_rows = rows + rows // 2 + 8
    vmem = pl.BlockSpec(memory_space=pltpu.VMEM)
    smem = pl.BlockSpec(memory_space=pltpu.SMEM)
    hbm = pl.BlockSpec(memory_space=pltpu.HBM)
    params = pltpu.CompilerParams(vmem_limit_bytes=40 * 1024 * 1024)
    large = pltpu.CompilerParams(vmem_limit_bytes=60 * 1024 * 1024)

    def call(body, name, outs, ins, specs, params=params, out=vmem, **more):
        return pl.pallas_call(
            body,
            out_shape=tuple(jax.ShapeDtypeStruct(*o) for o in outs),
            in_specs=specs,
            out_specs=out if isinstance(out, tuple) else (out,) * len(outs),
            compiler_params=params,
            name=name,
            **more,
        )(*ins)

    x, h = jnp.swapaxes(emb, 1, 2), jnp.swapaxes(grad_comp, 1, 2)
    index = lax.axis_index("table").astype(jnp.int32).reshape(1)
    part = comp_rows * (width // LANES) + 8
    shapes = [
        ((tables, total_rows, LANES), BF16), ((count * depth, LANES), BF16), ((tables // 2, part, LANES), BF16)
    ]
    sent, both, give = call(
        lambda *refs: send_kernel(tables, *refs),
        "send",
        shapes,
        (index, x, h, grad_fm, proj.T, comp, slot),
        [smem] + [hbm] * 6,
        params=large,
        out=hbm,
        scratch_shapes=[
            pltpu.VMEM(x.shape, BF16),
            pltpu.VMEM(h.shape, BF16),
            pltpu.VMEM(grad_fm.shape, BF16),
            pltpu.VMEM((rank, width), BF16),
            pltpu.VMEM(comp.shape, BF16),
            pltpu.VMEM(slot.shape, jnp.int32),
            pltpu.VMEM((2, count * width // 2, 2 * LANES), BF16),
            pltpu.VMEM((count, width, LANES), BF16),
            pltpu.VMEM((count * depth, LANES), BF16),
            pltpu.VMEM((count, depth, LANES), BF16),
            pltpu.VMEM((count * width, LANES), F32),
            pltpu.VMEM((count * width, LANES), F32),
        ]
        + [pltpu.VMEM(*shapes[0]), pltpu.VMEM(*shapes[2])]
        + [pltpu.SemaphoreType.DMA((16 + tables,))],
    )
    def swap(array, offset, other_group=0):
        pairs = [
            (g * tables + i, (g ^ other_group) * tables + (i ^ offset)) for g in range(groups) for i in range(tables)
        ]
        return lax.ppermute(array, ("dp", "table"), pairs)

    bits = tables.bit_length() - 1
    taken = swap(give, tables // 2)
    got = lax.all_to_all(sent, "table", split_axis=0, concat_axis=0, tiled=True)
    keep, = call(
        lambda *refs: keep_kernel(tables, rank, *refs),
        "keep",
        [((tables // 2, part, LANES), F32)],
        (index, x, h, both),
        [smem] + [vmem] * 3,
    )
    sums = [keep, taken]
    for stage in STAGES(bits):
        size = sums[0].shape[0] >> len(stage)
        cross = stage == STAGES(bits)[CROSS] and groups == 2
        kinds = [F32] + [LAST] * (2 ** len(stage) - 1)
        parts = call(
            lambda *refs, stage=stage: split_kernel(stage, *refs),
            "split",
            [((size, part, LANES), kind) for kind in kinds],
            (index, *sums),
            [smem] + [vmem] * len(sums),
            cost_estimate=pl.CostEstimate(flops=10**11 if stage == STAGES(bits)[0] else 10**6, bytes_accessed=10**6, transcendentals=0),
        )
        sums = [p if o == 0 else swap(p, o << stage[0]) for o, p in enumerate(parts)]
        if cross:
            sums += [swap(p, o << stage[0], 1) for o, p in enumerate(parts)]
    step = 1
    while step < groups and groups != 2:
        keep, = call(add_kernel, "add", [(sums[0].shape, F32)], sums, [vmem] * len(sums))
        sums = [keep, swap(keep, 0, step)]
        step *= 2
    scale = 1.0 / math.sqrt(count * tables * groups * depth)
    row_grads, grad_proj, grad_comp_out = call(
        lambda *refs: receive_kernel(slot_count // BLOCKS, scale, rank, *refs),
        "receive",
        [((local, depth, slot_count), BF16), ((local, rank), F32), ((comp_rows, width), F32)],
        (got, counts, *sums),
        [vmem] * (2 + len(sums)),
        out=hbm,
        scratch_shapes=[
            pltpu.VMEM((local, depth, slot_count), BF16),
            pltpu.VMEM((local, rank), F32),
            pltpu.VMEM((comp_rows, width), F32),
            pltpu.SemaphoreType.DMA((local // 2 + 2,)),
        ],
    )
    return (jnp.swapaxes(row_grads, 1, 2)[None], grad_proj, grad_comp_out)


def solution(mesh):
    placed = (
        P(("dp", "table"), None, None),
        P(("dp", "table"), None),
        P(("dp", "table"), None, None),
        P(),
        P(),
        P(("dp", "table"), None),
        P("dp", "table"),
    )
    return jax.shard_map(
        shards,
        mesh=mesh,
        in_specs=placed,
        out_specs=(P("dp", "table", None, None), P("table", None), P("table", None)),
        check_vma=False,
    )
```

```python
import math

import jax
import jax.numpy as jnp
from jax import lax
from jax.experimental import pallas as pl
from jax.experimental.pallas import tpu as pltpu
from jax.sharding import PartitionSpec as P

BLOCKS = 4
F32 = jnp.float32
BF16 = jnp.bfloat16
LANES = 128
HALF = 64
CROSS = 1
LAST = F32


def STAGES(bits):
    return [[b] for b in range(bits - 1)]


def dot(a, b, ca, cb):
    return lax.dot_general(a, b, (((ca,), (cb,)), ((), ())), preferred_element_type=F32)


def iota(shape, dim):
    return lax.broadcasted_iota(jnp.int32, shape, dim)


def round_up(n, m):
    return -(-n // m) * m


def send_kernel(tables, index_ref, x_hbm, h_hbm, g_hbm, proj_hbm, comp_hbm, slot_hbm, out_hbm, keep_hbm, give_hbm,
                x_ref, h_ref, g_ref, proj_ref, comp_ref, slot_ref, spread, factors, both, swapped, main, rest, out_ref, keep_ref, give_ref, sems):
    count, depth, width = x_ref.shape
    rank = proj_ref.shape[0]
    comp_width = comp_ref.shape[0]
    local, comp_rows = width // tables, comp_width // tables
    block = 8 * rank
    window = 2 * LANES

    pairs = [(g_hbm, g_ref), (proj_hbm, proj_ref), (comp_hbm, comp_ref), (slot_hbm, slot_ref)]
    small = [pltpu.make_async_copy(a, b, sems.at[i]) for i, (a, b) in enumerate(pairs)]
    pieces = 2
    size = count // pieces

    def in_pieces(a, b, at):
        parts = [pl.ds(p * size, size) for p in range(pieces)]
        return [pltpu.make_async_copy(a.at[p], b.at[p], sems.at[at + i]) for i, p in enumerate(parts)]

    x_copies = in_pieces(x_hbm, x_ref, 8 + tables)
    h_copies = in_pieces(h_hbm, h_ref, 8 + tables + pieces)
    for copy in small[:2] + x_copies + h_copies + small[2:]:
        copy.start()
    sends = [pltpu.make_async_copy(out_ref.at[t], out_hbm.at[t], sems.at[8 + t]) for t in range(tables)]
    part_copies = [
        pltpu.make_async_copy(give_ref, give_hbm, sems.at[6]), pltpu.make_async_copy(keep_ref, keep_hbm, sems.at[7])
    ]

    row, col = iota((rank, LANES), 0), iota((rank, LANES), 1)
    eye = ((col == row) | (col == row + rank)).astype(F32)
    place = ((col == row + HALF) | (col == row + HALF + rank)).astype(BF16)
    sub, lane = iota((8, window), 0), iota((8, window), 1)
    folds, masks = [], []
    for start in (0, HALF):
        parts = [eye] * 8
        if start:
            parts = [jnp.zeros((start, LANES), F32)] + parts
        if window > start + block:
            parts = parts + [jnp.zeros((window - start - block, LANES), F32)]
        folds.append(jnp.concatenate(parts, axis=0).astype(BF16))
        masks.append((lane >= start + rank * sub) & (lane < start + rank * (sub + 1)))
    first = (iota((depth, LANES), 1) % HALF) < rank

    small[0].wait()
    small[1].wait()
    for a in range(width // 8):
        start, odd = (a * block) // LANES * LANES, a % 2
        piece = g_ref[:, start:start + window].astype(F32)
        for s in range(count):
            wide = jnp.broadcast_to(piece[s:s + 1, :], (8, window))
            spread[odd, s * (width // 2) + (a // 2) * 8:s * (width // 2) + (a // 2) * 8 + 8, :] = jnp.where(masks[odd], wide, 0.0).astype(BF16)
    placed_proj = dot(proj_ref[...], place, 0, 0)
    for s in range(count):
        lo, hi = s * (width // 2), (s + 1) * (width // 2)
        halves = [dot(spread[i, lo:hi, :], folds[i], 1, 0).reshape(width // 16, 8, LANES) for i in range(2)]
        columns = jnp.stack(halves, axis=1).reshape(width, LANES)
        factors[s] = (columns + placed_proj).astype(BF16)
    for copy in x_copies:
        copy.wait()
    for s in range(count):
        terms = dot(x_ref[s], factors[s], 1, 0)
        high = terms.astype(BF16).astype(F32)
        split = jnp.where(first, high, terms - high)
        both[s * depth:(s + 1) * depth, :] = split.astype(BF16)
        swapped[s] = pltpu.roll(split, HALF, 1).astype(BF16)
    for copy in h_copies:
        copy.wait()
    small[2].wait()
    small[3].wait()

    blocks = weight_blocks(tables, rank, x_ref, h_ref, both)
    low = index_ref[0] < tables // 2
    for i in range(tables // 2):
        near, far = blocks[i], blocks[i + tables // 2]
        keep_ref[i] = jnp.where(low, near, far)
        give_ref[i] = jnp.where(low, far, near).astype(BF16)
    for copy in part_copies:
        copy.start()

    comp_t = comp_ref[...].astype(F32).T.astype(BF16)
    slot = slot_ref[...]
    slot_high = slot // 16
    sources = [slot_high.astype(F32), (slot - 16 * slot_high).astype(F32)]
    rows = local * count
    left = iota((rows // 2, LANES), 1) < HALF
    span = width
    for part in range(1):
        begin, end = part * span, (part + 1) * span
        for s in range(count):
            h, other = h_ref[s], swapped[s]
            h_wide = jnp.concatenate([h, h[LANES:]], axis=0)
            other_wide = jnp.concatenate([other, other[LANES:]], axis=0)
            grads = dot(comp_t[begin:end], h_wide, 1, 1) + dot(factors[s, begin:end], other_wide, 1, 1)
            main[pl.ds(begin * count + s, span, stride=count), :] = grads[:, :LANES]
            rest[pl.ds(begin * count + s, span, stride=count), :] = grads[:, LANES:]
        for t in range(part * tables, (part + 1) * tables):
            out_ref[t, 0:rows, :] = main[t * rows:(t + 1) * rows, :].astype(BF16)
            upper = rest[t * rows:t * rows + rows // 2, :]
            lower = rest[t * rows + rows // 2:(t + 1) * rows, :]
            out_ref[t, rows:rows + rows // 2, :] = jnp.where(left, upper, lower).astype(BF16)
            mixed = gather_lanes(sources, t, local)
            out_ref[t, rows + rows // 2:, :] = jnp.concatenate([mixed, mixed], axis=0).astype(BF16)
            sends[t].start()
    for copy in part_copies + sends:
        copy.wait()


def gather_lanes(sources, t, local):
    part, offset = (t * local) // LANES, (t * local) % LANES
    lane = iota((8, LANES), 1)
    mixed = jnp.zeros((8, LANES), F32)
    for i, source in enumerate(sources):
        piece = source[:, part * LANES:(part + 1) * LANES]
        shift = (i * local - offset) % LANES
        if shift:
            piece = pltpu.roll(piece, shift, 1)
        mixed = jnp.where((lane >= i * local) & (lane < (i + 1) * local), piece, mixed)
    return mixed


def weight_blocks(tables, rank, x_ref, h_ref, both):
    count, depth, width = x_ref.shape
    comp_width = h_ref.shape[2]
    local, comp_rows = width // tables, comp_width // tables
    x_all = x_ref[...].reshape(count * depth, width)
    h_all = h_ref[...].reshape(count * depth, comp_width)
    comp_grad = dot(h_all, x_all, 0, 0)
    proj_parts = dot(both[...], x_all, 0, 0)
    proj_grad = proj_parts[:rank] + proj_parts[rank:2 * rank]
    sources = [proj_grad[8 * i:8 * i + 8] for i in range(rank // 8)]

    def weight_block(t):
        mine = comp_grad[t * comp_rows:(t + 1) * comp_rows]
        pieces = [mine[:, i * LANES:(i + 1) * LANES] for i in range(width // LANES)]
        pieces.append(gather_lanes(sources, t, local))
        used = comp_rows * (width // LANES) + 8
        if used % 16:
            pieces.append(jnp.zeros((16 - used % 16, LANES), F32))
        return jnp.concatenate(pieces, axis=0)

    return [weight_block(t) for t in range(tables)]


def split(blocks, bits, index):
    if not bits:
        return [blocks]
    even = ((index >> bits[0]) % 2) == 0
    keep = [jnp.where(even, zero, one) for zero, one in zip(blocks[0::2], blocks[1::2])]
    give = [jnp.where(even, one, zero) for zero, one in zip(blocks[0::2], blocks[1::2])]
    return [part for pair in zip(split(keep, bits[1:], index), split(give, bits[1:], index)) for part in pair]


def total_of(refs, i):
    parts = [ref[i].astype(F32) for ref in refs]
    while len(parts) > 1:
        parts = [sum(parts[j:j + 2][1:], parts[j]) for j in range(0, len(parts), 2)]
    return parts[0]


def split_kernel(bits, index_ref, *refs):
    ins, outs = refs[:-2 ** len(bits)], refs[-2 ** len(bits):]
    parts = split([total_of(ins, i) for i in range(ins[0].shape[0])], bits, index_ref[0])
    for out, blocks in zip(outs, parts):
        for i, block in enumerate(blocks):
            out[i] = block.astype(out.dtype)


def add_kernel(*refs):
    refs[-1][0] = total_of(refs[:-1], 0)


def write_weights(scale, comp_rows, local, rank, refs, proj_ref, comp_ref):
    total = total_of(refs, 0) * scale
    halves = comp_ref.shape[1] // LANES
    comp_ref[...] = jnp.concatenate([total[i * comp_rows:(i + 1) * comp_rows] for i in range(halves)], axis=1)
    mixed = total[halves * comp_rows:halves * comp_rows + 8].T
    proj_ref[...] = jnp.concatenate([mixed[i * local:(i + 1) * local, :] for i in range(rank // 8)], axis=1)


def hold_kernel(in_ref, out_ref):
    pass


def receive_kernel(block_rows, scale, rank, in_ref, counts_ref, *refs):
    sums, (rows_hbm, proj_hbm, comp_hbm, rows_ref, proj_ref, comp_ref, sems) = refs[:-7], refs[-7:]
    write_weights(scale, comp_ref.shape[0], rows_ref.shape[0], rank, sums, proj_ref, comp_ref)
    pairs = rows_ref.shape[0] // 2
    weights = [
        pltpu.make_async_copy(proj_ref, proj_hbm, sems.at[pairs]),
        pltpu.make_async_copy(comp_ref, comp_hbm, sems.at[pairs + 1]),
    ]
    for copy in weights:
        copy.start()
    copies = []
    tables = in_ref.shape[0]
    local, depth, slots = rows_ref.shape
    count = 8
    rows = local * count
    tail = rows + rows // 2
    mixed = in_ref[:, tail:, :].astype(F32)[:, :8, :]
    slot = 16.0 * mixed[:, :, 0:local] + mixed[:, :, local:2 * local]
    limits = (counts_ref[...] * block_rows).astype(F32)
    slot = jnp.where(slot < limits[None], slot, -1.0)
    target = iota((tables, count, 2 * slots), 2)
    targets = [target.astype(F32), jnp.where(target < slots, -2, target - slots).astype(F32)]
    half_pairs = max(local // 4, 1)
    for j in range(local // 2):
        hot = jnp.stack(
            [(slot[:, :, 2 * j + i:2 * j + i + 1] == targets[i]).astype(F32) for i in range(2)], axis=1
        ).reshape(tables * 2 * count, 2 * slots).astype(BF16)
        lead = in_ref[:, 16 * j:16 * j + 16, :].reshape(tables * 16, LANES)
        k = j % half_pairs
        other = in_ref[:, rows + 16 * k:rows + 16 * k + 16, :].reshape(tables * 16, LANES)
        top = dot(lead, hot, 0, 0).astype(BF16)
        bottom = dot(other, hot, 0, 0)
        at = HALF * (j // half_pairs)
        bottom = bottom[at:at + HALF].astype(BF16)
        for i in range(2):
            rows_ref[2 * j + i, 0:LANES, :] = top[:, i * slots:(i + 1) * slots]
            rows_ref[2 * j + i, LANES:, :] = bottom[:, i * slots:(i + 1) * slots]
        pair = pl.ds(2 * j, 2)
        copies.append(pltpu.make_async_copy(rows_ref.at[pair], rows_hbm.at[pair], sems.at[j]))
        copies[j].start()
    for copy in copies + weights:
        copy.wait()


def shards(emb, grad_fm, grad_comp, proj, comp, slot, counts):
    count, width, depth = emb.shape
    rank = proj.shape[1]
    tables = lax.axis_size("table")
    groups = lax.axis_size("dp")
    local = width // tables
    slot_count = count * tables
    comp_width = comp.shape[0]
    comp_rows = comp_width // tables
    rows = local * count
    total_rows = rows + rows // 2 + 16
    vmem = pl.BlockSpec(memory_space=pltpu.VMEM)
    smem = pl.BlockSpec(memory_space=pltpu.SMEM)
    hbm = pl.BlockSpec(memory_space=pltpu.HBM)
    params = pltpu.CompilerParams(vmem_limit_bytes=40 * 1024 * 1024)
    large = pltpu.CompilerParams(vmem_limit_bytes=60 * 1024 * 1024)

    def call(body, name, outs, ins, specs, params=params, out=vmem, **more):
        return pl.pallas_call(
            body,
            out_shape=tuple(jax.ShapeDtypeStruct(*o) for o in outs),
            in_specs=specs,
            out_specs=out if isinstance(out, tuple) else (out,) * len(outs),
            compiler_params=params,
            name=name,
            **more,
        )(*ins)

    x, h = jnp.swapaxes(emb, 1, 2), jnp.swapaxes(grad_comp, 1, 2)
    index = lax.axis_index("table").astype(jnp.int32).reshape(1)
    part = round_up(comp_rows * (width // LANES) + 8, 16)
    shapes = [
        ((tables, total_rows, LANES), BF16), ((tables // 2, part, LANES), F32), ((tables // 2, part, LANES), BF16)
    ]
    sent, keep, give = call(
        lambda *refs: send_kernel(tables, *refs),
        "send",
        shapes,
        (index, x, h, grad_fm, proj.T, comp, slot),
        [smem] + [hbm] * 6,
        params=large,
        out=hbm,
        scratch_shapes=[
            pltpu.VMEM(x.shape, BF16),
            pltpu.VMEM(h.shape, BF16),
            pltpu.VMEM(grad_fm.shape, BF16),
            pltpu.VMEM((rank, width), BF16),
            pltpu.VMEM(comp.shape, BF16),
            pltpu.VMEM(slot.shape, jnp.int32),
            pltpu.VMEM((2, count * width // 2, 2 * LANES), BF16),
            pltpu.VMEM((count, width, LANES), BF16),
            pltpu.VMEM((count * depth, LANES), BF16),
            pltpu.VMEM((count, depth, LANES), BF16),
            pltpu.VMEM((count * width, LANES), F32),
            pltpu.VMEM((count * width, LANES), F32),
        ]
        + [pltpu.VMEM(*o) for o in shapes]
        + [pltpu.SemaphoreType.DMA((16 + tables,))],
    )
    def swap(array, offset, other_group=0):
        pairs = [
            (g * tables + i, (g ^ other_group) * tables + (i ^ offset)) for g in range(groups) for i in range(tables)
        ]
        return lax.ppermute(array, ("dp", "table"), pairs)

    bits = tables.bit_length() - 1
    sums = [keep, swap(give, tables // 2)]
    got = lax.all_to_all(sent, "table", split_axis=0, concat_axis=0, tiled=True)
    for stage in STAGES(bits):
        size = sums[0].shape[0] >> len(stage)
        cross = stage == STAGES(bits)[CROSS] and groups == 2
        kinds = [F32] + [LAST] * (2 ** len(stage) - 1)
        parts = call(
            lambda *refs, stage=stage: split_kernel(stage, *refs),
            "split",
            [((size, part, LANES), kind) for kind in kinds],
            (index, *sums),
            [smem] + [vmem] * len(sums),
            cost_estimate=pl.CostEstimate(flops=10**11 if stage == STAGES(bits)[0] else 10**6, bytes_accessed=10**6, transcendentals=0),
        )
        sums = [p if o == 0 else swap(p, o << stage[0]) for o, p in enumerate(parts)]
        if cross:
            sums += [swap(p, o << stage[0], 1) for o, p in enumerate(parts)]
    step = 1
    while step < groups and groups != 2:
        keep, = call(add_kernel, "add", [(sums[0].shape, F32)], sums, [vmem] * len(sums))
        sums = [keep, swap(keep, 0, step)]
        step *= 2
    scale = 1.0 / math.sqrt(count * tables * groups * depth)
    row_grads, grad_proj, grad_comp_out = call(
        lambda *refs: receive_kernel(slot_count // BLOCKS, scale, rank, *refs),
        "receive",
        [((local, depth, slot_count), BF16), ((local, rank), F32), ((comp_rows, width), F32)],
        (got, counts, *sums),
        [vmem] * (2 + len(sums)),
        out=hbm,
        scratch_shapes=[
            pltpu.VMEM((local, depth, slot_count), BF16),
            pltpu.VMEM((local, rank), F32),
            pltpu.VMEM((comp_rows, width), F32),
            pltpu.SemaphoreType.DMA((local // 2 + 2,)),
        ],
    )
    return (jnp.swapaxes(row_grads, 1, 2)[None], grad_proj, grad_comp_out)


def solution(mesh):
    placed = (
        P(("dp", "table"), None, None),
        P(("dp", "table"), None),
        P(("dp", "table"), None, None),
        P(),
        P(),
        P(("dp", "table"), None),
        P("dp", "table"),
    )
    return jax.shard_map(
        shards,
        mesh=mesh,
        in_specs=placed,
        out_specs=(P("dp", "table", None, None), P("table", None), P("table", None)),
        check_vma=False,
    )
```
